32 devices in a mesh: rep: 1, ep: 32 (over z, y, x, core).
Axes of the slice: x: 2, y: 2, z: 4, core: 2. Of those that a mesh axis runs over, the one named last changes fastest.
Arguments:
- tokens: bfloat16 [4096, 3584], P(('rep', 'ep')), may hold values from -6 to 6
- route_token: int32 [2048], P(('rep', 'ep')), may hold values from 0 to 127
- route_expert: int32 [2048, 1], P(('rep', 'ep')), may hold values from 0 to 3; in each aligned block of 64 rows (0 to 63, 64 to 127, ...) at most 24 rows name the same one
- route_gate: float32 [2048], P(('rep', 'ep')), may hold values from 0.25 to 2.5
- w_in: bfloat16 [32, 3584, 256], P('ep'), may hold values from -0.09375 to 0.09375
- w_out: bfloat16 [32, 128, 3584], P('ep'), may hold values from -0.1875 to 0.1875
- swap_pairs: int32 [16], replicated, may hold values 0 or 1
Outputs:
- mixed: bfloat16 [4096, 3584], P(('rep', 'ep'))
- saved_hidden: bfloat16 [32, 768, 128], P(('rep', 'ep'))
The draws below stay inside these ranges and needn't reach their ends.
Inputs may be any that keep to these rules, and one draw needn't show every extreme that they name: `route_expert`: in each block of 64 rows (the rows of one device) no expert is named by more than 24 rows, and some block names an expert exactly 24 times.
All inputs are finite; a program needn't handle non-finite values.
Results may differ from the reference program's by a relative error of at most 0.0057.
Values may be sent and summed in bfloat16 or wider, within the bound.
No kernel may reach another device: no remote copies, remote signals or barrier semaphores. Data moves between devices by JAX's collectives and lax.ppermute only.
A program may use at most 64 MiB of HBM per device.

```python
import math
import jax
import jax.numpy as jnp
import numpy as np
from jax import lax

D = 3584
HS = 128
SLICES = 8
TOK_DEV = 128
R_DEV = 64
HIDDEN_SIZE = 1024
EXPERTS = 4
C = 24
TOKENS = 4096
ROWS = 2048
N_EP = 32


def place_ends(entries, key, smallest, top_value):
    longest = entries.shape.index(max(entries.shape))
    spots = []
    for shift in (0, 1):
        where = [jax.random.randint(jax.random.fold_in(key, axis), (), 0, length) for axis, length in enumerate(entries.shape)]
        where[longest] = (where[longest] + shift) % entries.shape[longest]
        spots.append(tuple(where))
    return entries.at[spots[0]].set(smallest).at[spots[1]].set(top_value)


def levels(own_key, extent, shards, least, high):
    factor_of = 1.0
    for axis_at, parts in shards:
        steps = jax.random.uniform(jax.random.fold_in(jax.random.fold_in(own_key, 6), axis_at), (parts,), jnp.float32, least / len(shards), high / len(shards))
        factor_of = factor_of * jnp.repeat(jnp.exp(steps), extent[axis_at] // parts).reshape((-1,) + (1,) * (len(extent) - 1 - axis_at))
    return factor_of


def deal_out(stream_key, own, number, rows, number_of, top, reach, slope):
    order = jax.random.permutation(stream_key, number_of)
    packed, common = portions_of(number_of, rows * top, reach, slope, True), portions_of(number_of, rows * top, reach, slope, False)
    places = jnp.arange(number_of)

    def named(tallies, turn):
        used = int((tallies > 0).sum())
        fixed = max(1, used // 4)
        passed = fixed + (places - fixed + turn * (used - fixed)) % max(1, number_of - fixed)
        return jnp.zeros((number_of,), jnp.int32).at[order[jnp.where(places < fixed, places, passed)]].set(jnp.asarray(tallies, jnp.int32))

    tallies = jnp.where(number % 4 == 0, named(packed, number // 4), named(common, number - number // 4 - 1))
    mixed = jax.random.permutation(jax.random.fold_in(own, 3), number_of)
    donor, taker = mixed[0:number_of // 2 * 2:2], mixed[1:number_of // 2 * 2:2]
    slack = jnp.minimum(tallies[donor] - 1, reach - tallies[taker]) // 2
    slack = jnp.where((donor == order[0]) | (taker == order[0]) | (tallies[taker] == 0), 0, jnp.maximum(slack, 0))
    passed = jax.random.randint(jax.random.fold_in(own, 4), (number_of // 2,), 0, 1 << 20) % (slack + 1)
    tallies = tallies.at[donor].add(-passed).at[taker].add(passed)
    items = jnp.searchsorted(jnp.cumsum(tallies), jnp.arange(rows * top), side="right").astype(jnp.int32)
    table = items.reshape(top, rows).T
    table = table[jax.random.permutation(jax.random.fold_in(own, 1), rows)]
    turn = jax.random.randint(jax.random.fold_in(own, 2), (rows, 1), 0, top)
    return jnp.take_along_axis(table, (jnp.arange(top)[None, :] + turn) % top, axis=1)


def portions_of(count, total, reach, lean, full):
    weights = [(1 << 20) // math.isqrt(grade ** lean) + 1 for grade in range(1, count + 1)]
    largest = reach if full else min(reach, max(-(-total // count), total * weights[0] // sum(weights)))
    least = 1 if total - largest >= count - 1 else 0
    holding, surplus = [largest] + [least] * (count - 1), total - largest - least * (count - 1)
    while surplus > 0:
        candidates = [i for i in range(1, count) if holding[i] < largest] or [i for i in range(1, count) if holding[i] < reach]
        pool, left = sum([weights[i] for i in candidates]), surplus
        for i in candidates:
            addition = min(reach - holding[i], max(1, left * weights[i] // pool), surplus)
            holding[i] = holding[i] + addition
            surplus = surplus - addition
    return np.array(holding)


def bell_draw(own_key, dims, width, bound, cuts=(), held_as=jnp.bfloat16):
    drawn = width * jax.random.normal(own_key, dims, jnp.float32)
    if cuts:
        drawn = drawn * levels(own_key, dims, cuts, -0.22, 0.18)
    return jnp.clip(drawn, -bound, bound).astype(held_as)


def setup_inputs(seed: int = 0, part: int = 0) -> dict:
    splits = jax.random.split(jax.random.key(seed), 8)
    part_splits = jax.random.split(jax.random.fold_in(splits[7], part), 8)
    tokens = bell_draw(part_splits[0], (TOKENS, D), 1.0, 6.0, ((0, 32),))
    route_token = place_ends(jax.random.randint(part_splits[1], (ROWS,), 0, TOK_DEV), jax.random.fold_in(part_splits[1], 1), 0, TOK_DEV - 1).astype(jnp.int32)
    route_expert_keys = jax.random.split(jax.random.fold_in(part_splits[2], 1), ROWS // R_DEV)
    route_expert_turns = jax.random.permutation(jax.random.fold_in(part_splits[2], 3), ROWS // R_DEV)
    route_expert = jax.vmap(lambda own, number: deal_out(jax.random.fold_in(part_splits[2], 2), own, number, R_DEV, EXPERTS, 1, C, 1))(route_expert_keys, route_expert_turns).reshape((ROWS, 1))
    route_gate = jnp.clip(0.25 + 2.25 * jax.random.uniform(part_splits[3], (ROWS,), jnp.float32) ** levels(part_splits[3], (ROWS,), ((0, 32),), -0.2, 0.2), 0.25, 2.5)
    w_in = bell_draw(splits[4], (N_EP, D, 2 * HS), D ** -0.5, 0.09375, ((0, 32),))
    w_out = bell_draw(splits[5], (N_EP, HS, D), HIDDEN_SIZE ** -0.5, 0.1875, ((0, 32),))
    swap_pairs = place_ends((jax.random.randint(splits[6], (N_EP // 2,), 0, 2) < 1).astype(jnp.int32), jax.random.fold_in(splits[6], 1), 0, 1)
    return dict(tokens=tokens, route_token=route_token, route_expert=route_expert, route_gate=route_gate, w_in=w_in, w_out=w_out, swap_pairs=swap_pairs)


def pick_rows(local_block, index_block):
    return local_block[index_block]


def reference(tokens, route_token, route_expert, route_gate, w_in, w_out, swap_pairs):
    expert_ids = route_expert[:, 0].reshape(N_EP, R_DEV)
    token_ids = route_token.reshape(N_EP, R_DEV)
    expert_range = jnp.arange(EXPERTS, dtype=jnp.int32)
    slot_range = jnp.arange(C, dtype=jnp.int32)
    expert_hits = (expert_ids[:, :, None] == expert_range[None, None, :]).astype(jnp.int32)
    slot_index = jnp.sum((jnp.cumsum(expert_hits, axis=1) - 1) * expert_hits, axis=2)
    slot_table = ((expert_ids[:, None, None, :] == expert_range[None, :, None, None])
                  & (slot_index[:, None, None, :] == slot_range[None, None, :, None])).astype(jnp.float32)
    local_tokens = tokens.reshape(N_EP, TOK_DEV, D)
    picked = jax.vmap(pick_rows)(local_tokens, token_ids).astype(jnp.float32)
    expert_buf = jnp.einsum("qecr,qrd->eqcd", slot_table, picked, precision=lax.Precision.HIGHEST)
    expert_buf = expert_buf.astype(jnp.bfloat16).reshape(EXPERTS, N_EP * C, D)

    def block_step(totals, block_index):
        expert_index = block_index // SLICES
        inputs = lax.dynamic_index_in_dim(expert_buf, expert_index, 0, keepdims=False)
        weight_in = lax.dynamic_index_in_dim(w_in, block_index, 0, keepdims=False)
        weight_out = lax.dynamic_index_in_dim(w_out, block_index, 0, keepdims=False)
        gate_up = jnp.dot(inputs, weight_in, preferred_element_type=jnp.float32)
        hidden = (jax.nn.silu(gate_up[:, :HS]) * gate_up[:, HS:]).astype(jnp.bfloat16)
        partial_value = jnp.dot(hidden, weight_out, preferred_element_type=jnp.float32).astype(jnp.bfloat16)
        totals = totals.at[expert_index].add(partial_value.astype(jnp.float32))
        return totals, hidden

    start = jnp.zeros((EXPERTS, N_EP * C, D), jnp.float32)
    combined, hiddens = lax.scan(block_step, start, jnp.arange(N_EP, dtype=jnp.int32))
    flat_out = combined.reshape(EXPERTS * N_EP * C, D)
    device_ids = jnp.arange(N_EP, dtype=jnp.int32)
    flat_index = (expert_ids * (N_EP * C) + device_ids[:, None] * C + slot_index).reshape(-1)
    row_values = flat_out[flat_index]
    weighted = route_gate[:, None] * row_values
    token_index = (device_ids[:, None] * TOK_DEV + token_ids).reshape(-1)
    mixed = jax.ops.segment_sum(weighted, token_index, num_segments=TOKENS).astype(jnp.bfloat16)
    half_axis = N_EP // 2
    pair_flag = swap_pairs[device_ids % half_axis]
    served_block = jnp.where(pair_flag == 1, (device_ids + half_axis) % N_EP, device_ids)
    saved_hidden = hiddens[served_block]
    return mixed, saved_hidden
```

```python
import functools

import jax
import jax.numpy as jnp
from jax import lax
from jax.experimental import pallas as pl
from jax.experimental.pallas import tpu as pltpu
from jax.sharding import PartitionSpec as P

SLICES = 8
CORE, FIRST, SECOND = 1, 2, 4
VMEM = pl.BlockSpec(memory_space=pltpu.VMEM)
SMEM = pl.BlockSpec(memory_space=pltpu.SMEM)
VMEM_LIMIT = 48 * 1024 * 1024


def swap(value, mask_of):
    count = lax.axis_size("ep")
    return lax.ppermute(value, "ep", [(i, i ^ mask_of(i)) for i in range(count)])


def lane(i):
    return FIRST if i & CORE == 0 else SECOND


def cross(i):
    return SECOND if i & CORE == 0 else FIRST


def column_tile(width):
    return next(t for t in (512, 256, 128, width) if width % t == 0)


def route_kernel(experts, capacity, layer_ref, expert_ref, token_ref, gate_ref, tok_ref, *outs):
    bufs, (hi_ref, lo_ref) = outs[:experts], outs[experts:]
    rows = expert_ref.shape[1]
    tok_count, width = tok_ref.shape
    places = experts * capacity
    relative = expert_ref[...] ^ layer_ref[0]
    ranks = -(-experts // 8) * 8
    hits = (lax.broadcasted_iota(jnp.int32, (ranks, rows), 0) == relative).astype(jnp.float32)
    earlier = lax.broadcasted_iota(jnp.int32, (rows, rows), 0) < lax.broadcasted_iota(
        jnp.int32, (rows, rows), 1
    )
    before = jnp.dot(
        hits.astype(jnp.bfloat16),
        earlier.astype(jnp.float32).astype(jnp.bfloat16),
        preferred_element_type=jnp.float32,
    )
    slot = jnp.sum(hits * before, axis=0, keepdims=True).astype(jnp.int32)
    target = relative * capacity + slot
    place_hot = (lax.broadcasted_iota(jnp.int32, (places, rows), 0) == target).astype(jnp.float32)
    token_hot = (lax.broadcasted_iota(jnp.int32, (tok_count, rows), 0) == token_ref[...]).astype(
        jnp.float32
    )
    place_hot = place_hot.astype(jnp.bfloat16)
    gate = gate_ref[...]
    gate_hi = gate.astype(jnp.bfloat16).astype(jnp.float32)
    gate_lo = gate - gate_hi
    contract = (((1,), (1,)), ((), ()))
    for part, ref in ((gate_hi, hi_ref), (gate_lo, lo_ref)):
        ref[...] = lax.dot_general(
            (token_hot * part).astype(jnp.bfloat16),
            place_hot,
            contract,
            preferred_element_type=jnp.float32,
        ).astype(jnp.bfloat16)
    pick = lax.dot_general(
        place_hot, token_hot.astype(jnp.bfloat16), contract, preferred_element_type=jnp.float32
    ).astype(jnp.bfloat16)
    tile = column_tile(width)
    for at in range(0, width, tile):
        picked = jnp.dot(pick, tok_ref[:, at : at + tile], preferred_element_type=jnp.float32)
        for s in range(experts):
            bufs[s][:, at : at + tile] = picked[s * capacity : (s + 1) * capacity].astype(
                jnp.bfloat16
            )


def expert_kernel(count, place_ref, *refs):
    pieces = refs[:count]
    win_a, win_b, wout_a, wout_b = refs[count : count + 4]
    outs = refs[count + 4 : 2 * count + 4]
    hid_a, hid_b = refs[2 * count + 4 : 2 * count + 6]
    rows_ref, acc_ref, hidden_ref, wout_ref = refs[2 * count + 6 :]
    capacity, width = pieces[0].shape
    units = wout_a.shape[0]
    tile = column_tile(width)
    wout_ref[:units] = wout_a[...]
    wout_ref[units:] = wout_b[...]
    acc_ref[...] = jnp.zeros_like(acc_ref)

    @pl.loop(0, width // tile)
    def _(k):
        cols = pl.ds(pl.multiple_of(k * tile, tile), tile)
        rows_ref[...] = jnp.concatenate(
            [piece[:, cols].astype(jnp.float32) for piece in pieces], axis=0
        ).astype(jnp.bfloat16)
        rows = rows_ref[...]
        acc_ref[:, : 2 * units] += jnp.dot(
            rows, win_a[cols, :], preferred_element_type=jnp.float32
        )
        acc_ref[:, 2 * units :] += jnp.dot(
            rows, win_b[cols, :], preferred_element_type=jnp.float32
        )

    for half, hid in ((0, hid_a), (1, hid_b)):
        base = 2 * units * half
        gate, up = acc_ref[:, base : base + units], acc_ref[:, base + units : base + 2 * units]
        value = gate / (1.0 + jnp.exp(-gate)) * up
        hidden_ref[:, units * half : units * (half + 1)] = value.astype(jnp.bfloat16)
        for i in range(count):
            hid[place_ref[i]] = value[i * capacity : (i + 1) * capacity].astype(jnp.bfloat16)

    @pl.loop(0, width // tile)
    def _(k):
        cols = pl.ds(pl.multiple_of(k * tile, tile), tile)
        out = jnp.dot(hidden_ref[...], wout_ref[:, cols], preferred_element_type=jnp.float32)
        for i in range(count):
            outs[i][:, cols] = out[i * capacity : (i + 1) * capacity].astype(jnp.bfloat16)


def mix_kernel(experts, hi_ref, lo_ref, *refs):
    own, came = refs[:3], refs[3 : 2 + experts]
    mixed_ref = refs[2 + experts]
    capacity, width = own[0].shape
    tile = column_tile(width)
    for at in range(0, width, tile):
        cols = slice(at, at + tile)
        local = sum(r[:, cols].astype(jnp.float32) for r in own).astype(jnp.bfloat16)
        values = [local.astype(jnp.float32)] + [r[:, cols].astype(jnp.float32) for r in came]
        rows = jnp.concatenate(values, axis=0).astype(jnp.bfloat16)
        total = jnp.dot(hi_ref[...], rows, preferred_element_type=jnp.float32)
        total += jnp.dot(lo_ref[...], rows, preferred_element_type=jnp.float32)
        mixed_ref[:, cols] = total.astype(jnp.bfloat16)


def shards(tokens, route_token, route_expert, route_gate, w_in, w_out, swap_pairs):
    devices = lax.axis_size("ep")
    half_axis = devices // 2
    tok_count, width = tokens.shape
    units = w_out.shape[1]
    rows_dev = route_token.shape[0]
    experts = devices // SLICES
    capacity = min(rows_dev, 3 * rows_dev // (2 * experts))
    places = experts * capacity
    me = lax.axis_index("ep")
    layer = me // SLICES
    flag = swap_pairs[me % half_axis]
    params = pltpu.CompilerParams(vmem_limit_bytes=VMEM_LIMIT)
    block = jax.ShapeDtypeStruct((capacity, width), jnp.bfloat16)

    win_b = swap(w_in[0], lambda i: CORE)
    wout_b = swap(w_out[0], lambda i: CORE)

    mix_shape = jax.ShapeDtypeStruct((tok_count, places), jnp.bfloat16)
    *bufs, gate_hi, gate_lo = pl.pallas_call(
        functools.partial(route_kernel, experts, capacity),
        out_shape=[block] * experts + [mix_shape] * 2,
        in_specs=[SMEM] + [VMEM] * 4,
        out_specs=[VMEM] * (experts + 2),
        compiler_params=params,
    )(
        layer.reshape(1),
        route_expert.reshape(1, rows_dev),
        route_token.reshape(1, rows_dev),
        route_gate.reshape(1, rows_dev),
        tokens,
    )

    pieces, spots = [], []
    chip = (me % SLICES) // 2
    lane_mask = jnp.where(me % 2 == 0, FIRST, SECOND) // 2
    cross_mask = jnp.where(me % 2 == 0, SECOND, FIRST) // 2
    for s in range(experts):
        mine = bufs[s] if s == 0 else swap(bufs[s], lambda i: SLICES * s)
        beside = swap(mine, lane)
        across = swap(mine, cross)
        corner = swap(beside, cross)
        pieces += [mine, beside, across, corner]
        row = (layer ^ s) * (SLICES // 2)
        spots += [
            row + chip,
            row + (chip ^ lane_mask),
            row + (chip ^ cross_mask),
            row + (chip ^ lane_mask ^ cross_mask),
        ]
    count = len(pieces)
    hid_shape = jax.ShapeDtypeStruct((count, capacity, units), jnp.bfloat16)
    flops = 2 * count * capacity * width * units * 6
    *outs, hid_a, hid_b = pl.pallas_call(
        functools.partial(expert_kernel, count),
        out_shape=[block] * count + [hid_shape] * 2,
        in_specs=[SMEM] + [VMEM] * (count + 4),
        out_specs=[VMEM] * (count + 2),
        scratch_shapes=[
            pltpu.VMEM((count * capacity, column_tile(width)), jnp.bfloat16),
            pltpu.VMEM((count * capacity, 4 * units), jnp.float32),
            pltpu.VMEM((count * capacity, 2 * units), jnp.bfloat16),
            pltpu.VMEM((2 * units, width), jnp.bfloat16),
        ],
        compiler_params=params,
        cost_estimate=pl.CostEstimate(
            flops=flops, bytes_accessed=20 * 1024 * 1024, transcendentals=0
        ),
    )(jnp.stack(spots).astype(jnp.int32), *pieces, w_in[0], win_b, w_out[0], wout_b)

    own, came = None, []
    for s in reversed(range(experts)):
        mine, beside, across, corner = outs[4 * s : 4 * s + 4]
        relay = beside.astype(jnp.float32) + swap(corner, cross).astype(jnp.float32)
        from_lane = swap(relay.astype(jnp.bfloat16), lane)
        from_cross = swap(across, cross)
        if s == 0:
            own = [mine, from_lane, from_cross]
        else:
            total = sum(v.astype(jnp.float32) for v in (mine, from_lane, from_cross))
            came.insert(0, swap(total.astype(jnp.bfloat16), lambda i: SLICES * s))

    mixed = pl.pallas_call(
        functools.partial(mix_kernel, experts),
        out_shape=jax.ShapeDtypeStruct((tok_count, width), jnp.bfloat16),
        in_specs=[VMEM] * (4 + experts),
        out_specs=VMEM,
        compiler_params=params,
    )(gate_hi, gate_lo, *own, *came)

    other = swap(hid_b, lambda i: CORE)
    far_own = swap(hid_a, lambda i: half_axis)
    far_other = swap(hid_b, lambda i: half_axis ^ CORE)
    kept = jnp.where(flag == 1, far_own, hid_a)
    rest = jnp.where(flag == 1, far_other, other)
    even = me % 2 == 0
    saved = jnp.stack([jnp.where(even, kept, rest), jnp.where(even, rest, kept)], axis=1)
    return (mixed, saved.reshape(1, devices * capacity, units))


def solution(mesh):
    return jax.shard_map(
        shards,
        mesh=mesh,
        in_specs=(
            P(("rep", "ep"), None),
            P(("rep", "ep")),
            P(("rep", "ep"), None),
            P(("rep", "ep")),
            P("ep", None, None),
            P("ep", None, None),
            P(),
        ),
        out_specs=(P(("rep", "ep"), None), P(("rep", "ep"), None, None)),
        check_vma=False,
    )
```

```python
import functools

import jax
import jax.numpy as jnp
from jax import lax
from jax.experimental import pallas as pl
from jax.experimental.pallas import tpu as pltpu
from jax.sharding import PartitionSpec as P

SLICES = 8
CORE, FIRST, SECOND = 1, 2, 4
ANY = pl.BlockSpec(memory_space=pl.ANY)
WHOLE = pl.BlockSpec()
SMEM = pl.BlockSpec(memory_space=pltpu.SMEM)
VMEM_LIMIT = 48 * 1024 * 1024


def swap(value, mask_of):
    count = lax.axis_size("ep")
    return lax.ppermute(value, "ep", [(i, i ^ mask_of(i)) for i in range(count)])


def lane(i):
    return FIRST if i & CORE == 0 else SECOND


def cross(i):
    return SECOND if i & CORE == 0 else FIRST


def column_tile(width):
    return next(t for t in (512, 256, 128, width) if width % t == 0)


def route_kernel(experts, capacity, layer_ref, expert_ref, token_ref, gate_ref, tok_ref, *outs):
    bufs, (hi_ref, lo_ref) = outs[:experts], outs[experts : experts + 2]
    pick_ref = outs[experts + 2]
    rows = expert_ref.shape[1]
    tok_count = tok_ref.shape[0]
    places = experts * capacity

    @pl.when(pl.program_id(0) == 0)
    def _():
        relative = expert_ref[...] ^ layer_ref[0]
        ranks = -(-experts // 8) * 8
        hits = (lax.broadcasted_iota(jnp.int32, (ranks, rows), 0) == relative).astype(jnp.float32)
        earlier = lax.broadcasted_iota(jnp.int32, (rows, rows), 0) < lax.broadcasted_iota(
            jnp.int32, (rows, rows), 1
        )
        before = jnp.dot(
            hits.astype(jnp.bfloat16),
            earlier.astype(jnp.float32).astype(jnp.bfloat16),
            preferred_element_type=jnp.float32,
        )
        slot = jnp.sum(hits * before, axis=0, keepdims=True).astype(jnp.int32)
        target = relative * capacity + slot
        place_hot = lax.broadcasted_iota(jnp.int32, (places, rows), 0) == target
        place_hot = place_hot.astype(jnp.float32).astype(jnp.bfloat16)
        token_hot = lax.broadcasted_iota(jnp.int32, (tok_count, rows), 0) == token_ref[...]
        token_hot = token_hot.astype(jnp.float32)
        gate = gate_ref[...]
        gate_hi = gate.astype(jnp.bfloat16).astype(jnp.float32)
        contract = (((1,), (1,)), ((), ()))
        for part, ref in ((gate_hi, hi_ref), (gate - gate_hi, lo_ref)):
            ref[...] = lax.dot_general(
                (token_hot * part).astype(jnp.bfloat16),
                place_hot,
                contract,
                preferred_element_type=jnp.float32,
            ).astype(jnp.bfloat16)
        pick_ref[...] = lax.dot_general(
            place_hot, token_hot.astype(jnp.bfloat16), contract, preferred_element_type=jnp.float32
        ).astype(jnp.bfloat16)

    picked = jnp.dot(pick_ref[...], tok_ref[...], preferred_element_type=jnp.float32)
    for s in range(experts):
        bufs[s][...] = picked[s * capacity : (s + 1) * capacity].astype(jnp.bfloat16)


def expert_kernel(capacity, place_ref, *refs):
    pieces, (win_a, win_b, wout_a, wout_b) = refs[:4], refs[4:8]
    outs, (hid_a, hid_b) = refs[8:12], refs[12:14]
    rows_ref, win_ref, wout_ref, hidden_ref, out_ref, in_sem, weight_sem, out_sem = refs[14:]
    step, width = pieces[0].shape
    units = wout_a.shape[0]
    tile = column_tile(width)
    tiles = width // tile
    loads, later = [], []
    for k in range(tiles):
        cols = pl.ds(k * tile, tile)
        loads.append(
            [
                pltpu.make_async_copy(
                    piece.at[:, cols], rows_ref.at[pl.ds(i * step, step), cols], in_sem.at[k, i]
                )
                for i, piece in enumerate(pieces)
            ]
            + [
                pltpu.make_async_copy(
                    w.at[cols, :], win_ref.at[cols, pl.ds(2 * units * i, 2 * units)], in_sem.at[k, 4 + i]
                )
                for i, w in enumerate((win_a, win_b))
            ]
        )
    for i, w in enumerate((wout_a, wout_b)):
        later.append(
            pltpu.make_async_copy(w, wout_ref.at[pl.ds(units * i, units), :], weight_sem.at[i])
        )
    for copy in sum(loads, []) + later:
        copy.start()
    total = jnp.zeros((4 * step, 4 * units), jnp.float32)
    for k in range(tiles):
        for copy in loads[k]:
            copy.wait()
        cols = pl.ds(k * tile, tile)
        total += jnp.dot(rows_ref[:, cols], win_ref[cols, :], preferred_element_type=jnp.float32)
    for half, hid in ((0, hid_a), (1, hid_b)):
        base = 2 * units * half
        gate, up = total[:, base : base + units], total[:, base + units : base + 2 * units]
        value = gate / (1.0 + jnp.exp(-gate)) * up
        hidden_ref[:, units * half : units * (half + 1)] = value.astype(jnp.bfloat16)
        for i in range(4 * step // capacity):
            hid[place_ref[i]] = value[i * capacity : (i + 1) * capacity].astype(jnp.bfloat16)
    for copy in later:
        copy.wait()
    stores = []
    for k in range(tiles):
        cols = pl.ds(k * tile, tile)
        out = jnp.dot(hidden_ref[...], wout_ref[:, cols], preferred_element_type=jnp.float32)
        out_ref[:, cols] = out.astype(jnp.bfloat16)
        for i in range(4):
            copy = pltpu.make_async_copy(
                out_ref.at[pl.ds(i * step, step), cols], outs[i].at[:, cols], out_sem.at[k, i]
            )
            copy.start()
            stores.append(copy)
    for copy in stores:
        copy.wait()


def mix_kernel(hi_ref, lo_ref, *refs):
    values = [r[...].astype(jnp.float32) for r in refs[:-1]]
    rows = jnp.concatenate(values, axis=0).astype(jnp.bfloat16)
    total = jnp.dot(hi_ref[...], rows, preferred_element_type=jnp.float32)
    total += jnp.dot(lo_ref[...], rows, preferred_element_type=jnp.float32)
    refs[-1][...] = total.astype(jnp.bfloat16)


def run_expert(capacity, places, pieces, weights):
    step, width = pieces[0].shape
    units = weights[2].shape[0]
    rows = 4 * step
    tile = column_tile(width)
    tiles = width // tile
    block = jax.ShapeDtypeStruct((step, width), jnp.bfloat16)
    hid = jax.ShapeDtypeStruct((rows // capacity, capacity, units), jnp.bfloat16)
    return pl.pallas_call(
        functools.partial(expert_kernel, capacity),
        out_shape=[block] * 4 + [hid] * 2,
        in_specs=[SMEM] + [ANY] * 8,
        out_specs=[ANY] * 4 + [WHOLE] * 2,
        scratch_shapes=[
            pltpu.VMEM((rows, width), jnp.bfloat16),
            pltpu.VMEM((width, 4 * units), jnp.bfloat16),
            pltpu.VMEM((2 * units, width), jnp.bfloat16),
            pltpu.VMEM((rows, 2 * units), jnp.bfloat16),
            pltpu.VMEM((rows, width), jnp.bfloat16),
            pltpu.SemaphoreType.DMA((tiles, 6)),
            pltpu.SemaphoreType.DMA((2,)),
            pltpu.SemaphoreType.DMA((tiles, 4)),
        ],
        compiler_params=pltpu.CompilerParams(vmem_limit_bytes=VMEM_LIMIT),
        cost_estimate=pl.CostEstimate(
            flops=12 * rows * width * units, bytes_accessed=12 * 1024 * 1024, transcendentals=0
        ),
    )(places, *pieces, *weights)


def shards(tokens, route_token, route_expert, route_gate, w_in, w_out, swap_pairs):
    devices = lax.axis_size("ep")
    half_axis = devices // 2
    tok_count, width = tokens.shape
    units = w_out.shape[1]
    rows_dev = route_token.shape[0]
    experts = devices // SLICES
    capacity = min(rows_dev, 3 * rows_dev // (2 * experts))
    places = experts * capacity
    me = lax.axis_index("ep")
    layer = me // SLICES
    flag = swap_pairs[me % half_axis]
    params = pltpu.CompilerParams(vmem_limit_bytes=VMEM_LIMIT)
    block = jax.ShapeDtypeStruct((capacity, width), jnp.bfloat16)
    tile = column_tile(width)

    weights = [
        w_in[0],
        swap(w_in[0], lambda i: CORE),
        w_out[0],
        swap(w_out[0], lambda i: CORE),
    ]
    mix_shape = jax.ShapeDtypeStruct((tok_count, places), jnp.bfloat16)
    fixed = lambda shape: pl.BlockSpec(shape, lambda i: (0, 0))
    moving = lambda rows: pl.BlockSpec((rows, tile), lambda i: (0, i))
    *bufs, gate_hi, gate_lo = pl.pallas_call(
        functools.partial(route_kernel, experts, capacity),
        out_shape=[block] * experts + [mix_shape] * 2,
        grid=(width // tile,),
        in_specs=[SMEM] + [fixed((1, rows_dev))] * 3 + [moving(tok_count)],
        out_specs=[moving(capacity)] * experts + [fixed((tok_count, places))] * 2,
        scratch_shapes=[pltpu.VMEM((places, tok_count), jnp.bfloat16)],
        compiler_params=params,
    )(
        layer.reshape(1),
        route_expert.reshape(1, rows_dev),
        route_token.reshape(1, rows_dev),
        route_gate.reshape(1, rows_dev),
        tokens,
    )

    chip = (me % SLICES) // 2
    lane_mask = jnp.where(me % 2 == 0, FIRST, SECOND) // 2
    cross_mask = jnp.where(me % 2 == 0, SECOND, FIRST) // 2
    chips = [chip, chip ^ lane_mask, chip ^ cross_mask, chip ^ lane_mask ^ cross_mask]
    pairs = experts // 2
    sources = [bufs[0]] + [swap(bufs[s], lambda i: SLICES * s) for s in range(1, experts)]
    runs = []
    for pair in range(pairs):
        mine = jnp.concatenate(sources[2 * pair : 2 * pair + 2], axis=0)
        beside = swap(mine, lane)
        across = swap(mine, cross)
        corner = swap(beside, cross)
        spots = [((layer ^ s) % 2) * (SLICES // 2) + c for c in chips for s in (0, 1)]
        runs.append(
            run_expert(
                capacity, jnp.stack(spots).astype(jnp.int32), [mine, beside, across, corner], weights
            )
        )

    finals = [None] * experts
    for pair in reversed(range(pairs)):
        mine, beside, across, corner = runs[pair][:4]
        relay = beside.astype(jnp.float32) + swap(corner, cross).astype(jnp.float32)
        from_lane = swap(relay.astype(jnp.bfloat16), lane)
        from_cross = swap(across, cross)
        for part in (0, 1):
            s = 2 * pair + part
            rows = slice(part * capacity, (part + 1) * capacity)
            total = sum(v[rows].astype(jnp.float32) for v in (mine, from_lane, from_cross))
            total = total.astype(jnp.bfloat16)
            finals[s] = total if s == 0 else swap(total, lambda i: SLICES * s)

    mixed = pl.pallas_call(
        mix_kernel,
        out_shape=jax.ShapeDtypeStruct((tok_count, width), jnp.bfloat16),
        grid=(width // tile,),
        in_specs=[fixed((tok_count, places))] * 2 + [moving(capacity)] * experts,
        out_specs=moving(tok_count),
        compiler_params=params,
    )(gate_hi, gate_lo, *finals)

    by_pair = [[runs[p][4 + half] for p in range(pairs)] for half in (0, 1)]
    high = layer // 2
    ordered = [
        jnp.concatenate(
            [sum(jnp.where(high ^ p == q, part[q], 0) for q in range(pairs)) for p in range(pairs)],
            axis=0,
        )
        for part in by_pair
    ]
    other = swap(ordered[1], lambda i: CORE)
    even = me % 2 == 0
    full = jnp.stack(
        [jnp.where(even, ordered[0], other), jnp.where(even, other, ordered[0])], axis=1
    ).reshape(1, devices * capacity, units)
    far = swap(full, lambda i: half_axis)
    return (mixed, jnp.where(flag == 1, far, full))


def solution(mesh):
    return jax.shard_map(
        shards,
        mesh=mesh,
        in_specs=(
            P(("rep", "ep"), None),
            P(("rep", "ep")),
            P(("rep", "ep"), None),
            P(("rep", "ep")),
            P("ep", None, None),
            P("ep", None, None),
            P(),
        ),
        out_specs=(P(("rep", "ep"), None), P(("rep", "ep"), None, None)),
        check_vma=False,
    )
```

```python
import functools

import jax
import jax.numpy as jnp
from jax import lax
from jax.experimental import pallas as pl
from jax.experimental.pallas import tpu as pltpu
from jax.sharding import PartitionSpec as P

SLICES = 8
CORE, FIRST, SECOND = 1, 2, 4
CHIPS = SLICES // 2
VMEM = pl.BlockSpec(memory_space=pltpu.VMEM)
SMEM = pl.BlockSpec(memory_space=pltpu.SMEM)
ANY = pl.BlockSpec(memory_space=pl.ANY)
MIB = 1024 * 1024


def swap(value, mask_of):
    count = lax.axis_size("ep")
    return lax.ppermute(value, "ep", [(i, i ^ mask_of(i)) for i in range(count)])


def after(value, others):
    return lax.optimization_barrier((value, others))[0]


def lane(i):
    return FIRST if i & CORE == 0 else SECOND


def cross(i):
    return SECOND if i & CORE == 0 else FIRST


def column_tile(width):
    return next(t for t in (1792, 512, 256, 128, width) if width % t == 0)


def route_kernel(experts, capacity, me_ref, expert_hbm, token_hbm, gate_hbm, tok_hbm, *refs):
    bufs, (hi_ref, lo_ref) = refs[:experts], refs[experts : experts + 2]
    expert_ref, token_ref, gate_ref, tok_ref, out_ref, sems, out_sems = refs[experts + 2 :]
    rows = expert_ref.shape[1]
    tok_count, width = tok_ref.shape
    places = experts * capacity
    tile = column_tile(width)
    tiles = width // tile
    small = [
        pltpu.make_async_copy(source, target, sems.at[i])
        for i, (source, target) in enumerate(
            ((expert_hbm, expert_ref), (token_hbm, token_ref), (gate_hbm, gate_ref))
        )
    ]
    large = [
        pltpu.make_async_copy(
            tok_hbm.at[:, pl.ds(k * tile, tile)], tok_ref.at[:, pl.ds(k * tile, tile)], sems.at[3 + k]
        )
        for k in range(tiles)
    ]
    for copy in small + large:
        copy.start()
    for copy in small:
        copy.wait()
    relative = expert_ref[...] ^ (me_ref[0] // SLICES)
    ranks = -(-experts // 8) * 8
    hits = (lax.broadcasted_iota(jnp.int32, (ranks, rows), 0) == relative).astype(jnp.float32)
    earlier = lax.broadcasted_iota(jnp.int32, (rows, rows), 0) < lax.broadcasted_iota(
        jnp.int32, (rows, rows), 1
    )
    before = jnp.dot(
        hits.astype(jnp.bfloat16),
        earlier.astype(jnp.float32).astype(jnp.bfloat16),
        preferred_element_type=jnp.float32,
    )
    slot = jnp.sum(hits * before, axis=0, keepdims=True).astype(jnp.int32)
    target = relative * capacity + slot
    place_hot = lax.broadcasted_iota(jnp.int32, (places, rows), 0) == target
    place_hot = place_hot.astype(jnp.float32).astype(jnp.bfloat16)
    token_hot = lax.broadcasted_iota(jnp.int32, (tok_count, rows), 0) == token_ref[...]
    token_hot = token_hot.astype(jnp.float32)
    contract = (((1,), (1,)), ((), ()))
    pick = lax.dot_general(
        place_hot, token_hot.astype(jnp.bfloat16), contract, preferred_element_type=jnp.float32
    ).astype(jnp.bfloat16)
    stores = []
    for k in range(tiles):
        cols = pl.ds(k * tile, tile)
        large[k].wait()
        picked = jnp.dot(pick, tok_ref[:, cols], preferred_element_type=jnp.float32)
        for s in range(experts):
            out_ref[s, :, cols] = picked[s * capacity : (s + 1) * capacity].astype(jnp.bfloat16)
    for s in range(experts):
        copy = pltpu.make_async_copy(out_ref.at[s], bufs[s], out_sems.at[s])
        copy.start()
        stores.append(copy)
    gate = gate_ref[...]
    gate_hi = gate.astype(jnp.bfloat16).astype(jnp.float32)
    for part, ref in ((gate_hi, hi_ref), (gate - gate_hi, lo_ref)):
        ref[...] = lax.dot_general(
            (token_hot * part).astype(jnp.bfloat16),
            place_hot,
            contract,
            preferred_element_type=jnp.float32,
        ).astype(jnp.bfloat16)
    for copy in stores:
        copy.wait()


def run_route(experts, capacity, me, route_expert, route_token, route_gate, tokens):
    tok_count, width = tokens.shape
    rows = route_token.shape[0]
    block = jax.ShapeDtypeStruct((capacity, width), jnp.bfloat16)
    mix = jax.ShapeDtypeStruct((tok_count, experts * capacity), jnp.bfloat16)
    return pl.pallas_call(
        functools.partial(route_kernel, experts, capacity),
        out_shape=[block] * experts + [mix] * 2,
        in_specs=[SMEM] + [ANY] * 4,
        out_specs=[ANY] * experts + [VMEM] * 2,
        scratch_shapes=[
            pltpu.VMEM((1, rows), jnp.int32),
            pltpu.VMEM((1, rows), jnp.int32),
            pltpu.VMEM((1, rows), jnp.float32),
            pltpu.VMEM((tok_count, width), jnp.bfloat16),
            pltpu.VMEM((experts, capacity, width), jnp.bfloat16),
            pltpu.SemaphoreType.DMA((3 + width // column_tile(width),)),
            pltpu.SemaphoreType.DMA((experts,)),
        ],
        compiler_params=pltpu.CompilerParams(vmem_limit_bytes=60 * MIB),
    )(
        me,
        route_expert.reshape(1, rows),
        route_token.reshape(1, rows),
        route_gate.reshape(1, rows),
        tokens,
    )


def expert_kernel(chunks, backs, me_ref, *refs):
    count = 2 * len(chunks)
    pieces, (win_a, win_b, wout_a, wout_b) = refs[:count], refs[count : count + 4]
    outs, hids = refs[count + 4 : count + 4 + 2 * len(backs)], refs[count + 4 + 2 * len(backs) : -2]
    rows_ref, hidden_ref = refs[-2:]
    units, width = wout_a.shape
    capacity = hids[0].shape[1]
    tile = column_tile(width)
    at = 0
    for piece in pieces:
        rows_ref[at : at + piece.shape[0]] = piece[...]
        at += piece.shape[0]
    me = me_ref[0]
    layer, chip, core = me // SLICES, (me % SLICES) // 2, me % 2
    lane_mask = (FIRST + core * (SECOND - FIRST)) // 2
    cross_mask = (SECOND - core * (SECOND - FIRST)) // 2
    masks = (0, lane_mask, cross_mask, lane_mask ^ cross_mask)
    blocks = [(s, k) for chunk in chunks for k in range(4) for s in chunk]
    for half, (win, hid) in enumerate(zip((win_a, win_b), hids)):
        total = jnp.dot(rows_ref[...], win[...], preferred_element_type=jnp.float32)
        gate, up = total[:, :units], total[:, units:]
        value = (gate / (1.0 + jnp.exp(-gate)) * up).astype(jnp.bfloat16)
        hidden_ref[:, units * half : units * (half + 1)] = value
        value = value.astype(jnp.float32)
        for i, (s, k) in enumerate(blocks):
            hid[(layer ^ s) * CHIPS + (chip ^ masks[k])] = value[
                i * capacity : (i + 1) * capacity
            ].astype(jnp.bfloat16)
    for at in range(0, width, tile):
        cols = slice(at, at + tile)
        out = jnp.dot(hidden_ref[:, :units], wout_a[:, cols], preferred_element_type=jnp.float32)
        out += jnp.dot(hidden_ref[:, units:], wout_b[:, cols], preferred_element_type=jnp.float32)
        for i, ref in enumerate(outs):
            parts = []
            for k in (0, 1) if i % 2 == 0 else (2, 3):
                for s in backs[i // 2]:
                    start = blocks.index((s, k)) * capacity
                    parts.append(out[start : start + capacity])
            ref[:, cols] = jnp.concatenate(parts, axis=0).astype(jnp.bfloat16)


def run_expert(chunks, backs, capacity, me, pieces, weights):
    width = pieces[0].shape[1]
    units = weights[2].shape[0]
    rows = sum(piece.shape[0] for piece in pieces)
    hid = jax.ShapeDtypeStruct((rows // capacity, capacity, units), jnp.bfloat16)
    outs = [
        jax.ShapeDtypeStruct((2 * len(back) * capacity, width), jnp.bfloat16)
        for back in backs
        for _ in (0, 1)
    ]
    return pl.pallas_call(
        functools.partial(expert_kernel, chunks, backs),
        out_shape=outs + [hid] * 2,
        in_specs=[SMEM] + [VMEM] * (len(pieces) + 4),
        out_specs=[VMEM] * (len(outs) + 2),
        scratch_shapes=[
            pltpu.VMEM((rows, width), jnp.bfloat16),
            pltpu.VMEM((rows, 2 * units), jnp.bfloat16),
        ],
        compiler_params=pltpu.CompilerParams(vmem_limit_bytes=16 * MIB),
        cost_estimate=pl.CostEstimate(flops=1, bytes_accessed=1, transcendentals=0),
    )(me, *pieces, *weights)


def weave_kernel(me_ref, mine_ref, other_ref, out_ref):
    core = me_ref[0] % 2
    out_ref[:, pl.ds(core, 1)] = mine_ref[...][:, None]
    out_ref[:, pl.ds(1 - core, 1)] = other_ref[...][:, None]


def keep_kernel(me_ref, swap_ref, mine_ref, far_ref, out_ref):
    flag = swap_ref[me_ref[0] % swap_ref.shape[0]]
    out_ref[...] = jnp.where(flag == 1, far_ref[...], mine_ref[...])


def mix_kernel(hi_ref, lo_ref, *refs):
    values = [r[...].astype(jnp.float32) for r in refs[:-1]]
    rows = jnp.concatenate(values, axis=0).astype(jnp.bfloat16)
    total = jnp.dot(hi_ref[...], rows, preferred_element_type=jnp.float32)
    total += jnp.dot(lo_ref[...], rows, preferred_element_type=jnp.float32)
    refs[-1][...] = total.astype(jnp.bfloat16)


def shards(tokens, route_token, route_expert, route_gate, w_in, w_out, swap_pairs):
    devices = lax.axis_size("ep")
    half_axis = devices // 2
    tok_count, width = tokens.shape
    units = w_out.shape[1]
    rows_dev = route_token.shape[0]
    experts = devices // SLICES
    capacity = min(rows_dev, 3 * rows_dev // (2 * experts))
    places = experts * capacity
    me = lax.axis_index("ep").astype(jnp.int32).reshape(1)
    small = pltpu.CompilerParams(vmem_limit_bytes=16 * MIB)

    weights = [
        w_in[0],
        swap(w_in[0], lambda i: CORE),
        w_out[0],
        swap(w_out[0], lambda i: CORE),
    ]
    *bufs, gate_hi, gate_lo = run_route(
        experts, capacity, me, route_expert, route_token, route_gate, tokens
    )

    chunks = [[0], [1, experts - 1]] + [[s] for s in range(2, experts - 1)]
    backs = [[s] for s in reversed(range(experts))]
    received = {0: bufs[0]}
    gathered = {}
    ready = list(bufs)
    for c, chunk in enumerate(chunks):
        for s in chunk:
            if s:
                received[s] = swap(ready[s], lambda i: SLICES * s)
        if c == 1:
            kept = [received[s] for s in chunk]
            kept = after(kept, gathered[0][0])
            ready, kept = lax.optimization_barrier((ready, kept))
            for s, value in zip(chunk, kept):
                received[s] = value
        if c > 1:
            kept = after([received[s] for s in chunk], gathered[c - 1][0])
            received.update(zip(chunk, kept))
        mine = jnp.concatenate([received[s] for s in chunk], axis=0)
        beside = swap(mine, lane)
        both = jnp.concatenate([mine, beside], axis=0)
        gathered[c] = [both, swap(both, cross)]

    *outs, hid_a, hid_b = run_expert(
        chunks, backs, capacity, me, sum([gathered[c] for c in range(len(chunks))], []), weights
    )

    finals = [None] * experts
    lasts, got, totals = [], [], []
    for b, back in enumerate(backs):
        near, away = outs[2 * b : 2 * b + 2]
        half = near.shape[0] // 2
        if b > 1:
            away = after(away, got[b - 2])
        came = swap(away, cross)
        if b > 1:
            came = after(came, totals[b - 2 : b - 1])
        got.append(came)
        relay = near[half:].astype(jnp.float32) + came[half:].astype(jnp.float32)
        last = swap(relay.astype(jnp.bfloat16), lane)
        lasts.append(last)
        part = []
        for i, s in enumerate(back):
            rows = slice(i * capacity, (i + 1) * capacity)
            total = sum(v[rows].astype(jnp.float32) for v in (near, came, last))
            total = total.astype(jnp.bfloat16)
            part.append(total)
            finals[s] = total if s == 0 else swap(total, lambda i: SLICES * s)
        totals.append(part)

    tile = column_tile(width)
    moving = lambda rows: pl.BlockSpec((rows, tile), lambda i: (0, i))
    fixed = pl.BlockSpec((tok_count, places), lambda i: (0, 0))
    mixed = pl.pallas_call(
        mix_kernel,
        out_shape=jax.ShapeDtypeStruct((tok_count, width), jnp.bfloat16),
        grid=(width // tile,),
        in_specs=[fixed] * 2 + [moving(capacity)] * experts,
        out_specs=moving(tok_count),
        compiler_params=small,
    )(gate_hi, gate_lo, *finals)

    other = swap(hid_b, lambda i: CORE)
    full = pl.pallas_call(
        weave_kernel,
        out_shape=jax.ShapeDtypeStruct((devices // 2, 2, capacity, units), jnp.bfloat16),
        in_specs=[SMEM, VMEM, VMEM],
        out_specs=VMEM,
        compiler_params=small,
    )(me, hid_a, other)
    far = after(swap(full, lambda i: half_axis), lasts[:2])
    saved = pl.pallas_call(
        keep_kernel,
        out_shape=jax.ShapeDtypeStruct(full.shape, full.dtype),
        in_specs=[SMEM, SMEM, VMEM, VMEM],
        out_specs=pl.BlockSpec(),
        compiler_params=small,
    )(me, swap_pairs, full, far)
    return (mixed, saved.reshape(1, devices * capacity, units))


def solution(mesh):
    return jax.shard_map(
        shards,
        mesh=mesh,
        in_specs=(
            P(("rep", "ep"), None),
            P(("rep", "ep")),
            P(("rep", "ep"), None),
            P(("rep", "ep")),
            P("ep", None, None),
            P("ep", None, None),
            P(),
        ),
        out_specs=(P(("rep", "ep"), None), P(("rep", "ep"), None, None)),
        check_vma=False,
    )
```

```python
import functools

import jax
import jax.numpy as jnp
from jax import lax
from jax.experimental import pallas as pl
from jax.experimental.pallas import tpu as pltpu
from jax.sharding import PartitionSpec as P

SLICES = 8
CORE, FIRST, SECOND = 1, 2, 4
CHIPS = SLICES // 2
VMEM = pl.BlockSpec(memory_space=pltpu.VMEM)
SMEM = pl.BlockSpec(memory_space=pltpu.SMEM)
ANY = pl.BlockSpec(memory_space=pl.ANY)
MIB = 1024 * 1024


def swap(value, mask_of):
    count = lax.axis_size("ep")
    return lax.ppermute(value, "ep", [(i, i ^ mask_of(i)) for i in range(count)])


def after(value, others):
    return lax.optimization_barrier((value, others))[0]


def lane(i):
    return FIRST if i & CORE == 0 else SECOND


def cross(i):
    return SECOND if i & CORE == 0 else FIRST


def column_tile(width):
    return next(t for t in (1792, 512, 256, 128, width) if width % t == 0)


def route_kernel(experts, capacity, me_ref, expert_hbm, token_hbm, gate_hbm, tok_hbm, *refs):
    bufs, (hi_ref, lo_ref) = refs[:experts], refs[experts : experts + 2]
    expert_ref, token_ref, gate_ref, tok_ref, sems = refs[experts + 2 :]
    rows = expert_ref.shape[1]
    tok_count, width = tok_ref.shape
    places = experts * capacity
    tile = column_tile(width)
    tiles = width // tile
    small = [
        pltpu.make_async_copy(source, target, sems.at[i])
        for i, (source, target) in enumerate(
            ((expert_hbm, expert_ref), (token_hbm, token_ref), (gate_hbm, gate_ref))
        )
    ]
    large = [
        pltpu.make_async_copy(
            tok_hbm.at[:, pl.ds(k * tile, tile)], tok_ref.at[:, pl.ds(k * tile, tile)], sems.at[3 + k]
        )
        for k in range(tiles)
    ]
    for copy in small + large:
        copy.start()
    for copy in small:
        copy.wait()
    relative = expert_ref[...] ^ (me_ref[0] // SLICES)
    ranks = -(-experts // 8) * 8
    hits = (lax.broadcasted_iota(jnp.int32, (ranks, rows), 0) == relative).astype(jnp.float32)
    earlier = lax.broadcasted_iota(jnp.int32, (rows, rows), 0) < lax.broadcasted_iota(
        jnp.int32, (rows, rows), 1
    )
    before = jnp.dot(
        hits.astype(jnp.bfloat16),
        earlier.astype(jnp.float32).astype(jnp.bfloat16),
        preferred_element_type=jnp.float32,
    )
    slot = jnp.sum(hits * before, axis=0, keepdims=True).astype(jnp.int32)
    target = relative * capacity + slot
    place_hot = lax.broadcasted_iota(jnp.int32, (places, rows), 0) == target
    place_hot = place_hot.astype(jnp.float32).astype(jnp.bfloat16)
    token_hot = lax.broadcasted_iota(jnp.int32, (tok_count, rows), 0) == token_ref[...]
    token_hot = token_hot.astype(jnp.float32)
    contract = (((1,), (1,)), ((), ()))
    pick = lax.dot_general(
        place_hot, token_hot.astype(jnp.bfloat16), contract, preferred_element_type=jnp.float32
    ).astype(jnp.bfloat16)
    for k in range(tiles):
        cols = pl.ds(k * tile, tile)
        large[k].wait()
        picked = jnp.dot(pick, tok_ref[:, cols], preferred_element_type=jnp.float32)
        for s in range(experts):
            bufs[s][:, cols] = picked[s * capacity : (s + 1) * capacity].astype(jnp.bfloat16)
    gate = gate_ref[...]
    gate_hi = gate.astype(jnp.bfloat16).astype(jnp.float32)
    for part, ref in ((gate_hi, hi_ref), (gate - gate_hi, lo_ref)):
        ref[...] = lax.dot_general(
            (token_hot * part).astype(jnp.bfloat16),
            place_hot,
            contract,
            preferred_element_type=jnp.float32,
        ).astype(jnp.bfloat16)


def run_route(experts, capacity, me, route_expert, route_token, route_gate, tokens):
    tok_count, width = tokens.shape
    rows = route_token.shape[0]
    block = jax.ShapeDtypeStruct((capacity, width), jnp.bfloat16)
    mix = jax.ShapeDtypeStruct((tok_count, experts * capacity), jnp.bfloat16)
    return pl.pallas_call(
        functools.partial(route_kernel, experts, capacity),
        out_shape=[block] * experts + [mix] * 2,
        in_specs=[SMEM] + [ANY] * 4,
        out_specs=[VMEM] * (experts + 2),
        scratch_shapes=[
            pltpu.VMEM((1, rows), jnp.int32),
            pltpu.VMEM((1, rows), jnp.int32),
            pltpu.VMEM((1, rows), jnp.float32),
            pltpu.VMEM((tok_count, width), jnp.bfloat16),
            pltpu.SemaphoreType.DMA((3 + width // column_tile(width),)),
        ],
        compiler_params=pltpu.CompilerParams(vmem_limit_bytes=60 * MIB),
    )(
        me,
        route_expert.reshape(1, rows),
        route_token.reshape(1, rows),
        route_gate.reshape(1, rows),
        tokens,
    )


def expert_kernel(chunks, backs, ahead, final, me_ref, *refs):
    count = 2 * len(chunks)
    pieces, (win_a, win_b, wout_a, wout_b) = refs[:count], refs[count : count + 4]
    held, refs = refs[count + 4 : count + 4 + 2 * len(ahead)], refs[count + 4 + 2 * len(ahead) :]
    outs, hids = refs[: 2 * len(backs)], refs[2 * len(backs) : -2]
    rows_ref, hidden_ref = refs[-2:]
    units, width = wout_a.shape
    capacity = hids[0].shape[1]
    tile = column_tile(width)
    at = 0
    for piece in pieces:
        rows_ref[at : at + piece.shape[0]] = piece[...]
        at += piece.shape[0]
    me = me_ref[0]
    layer, chip, core = me // SLICES, (me % SLICES) // 2, me % 2
    lane_mask = (FIRST + core * (SECOND - FIRST)) // 2
    cross_mask = (SECOND - core * (SECOND - FIRST)) // 2
    masks = (0, lane_mask, cross_mask, lane_mask ^ cross_mask)
    blocks = [(s, k) for chunk in chunks for k in range(4) for s in chunk]

    def spot(s, k):
        return (layer ^ s) * CHIPS + (chip ^ masks[k])

    for e, earlier in enumerate(ahead):
        for half in (0, 1):
            for i, (s, k) in enumerate(earlier):
                hids[half][spot(s, k)] = held[2 * e + half][i]
    for half, (win, hid) in enumerate(zip((win_a, win_b), hids)):
        total = jnp.dot(rows_ref[...], win[...], preferred_element_type=jnp.float32)
        gate, up = total[:, :units], total[:, units:]
        value = (gate / (1.0 + jnp.exp(-gate)) * up).astype(jnp.bfloat16)
        hidden_ref[:, units * half : units * (half + 1)] = value
        value = value.astype(jnp.float32)
        for i, (s, k) in enumerate(blocks):
            hid[spot(s, k) if final else i] = value[
                i * capacity : (i + 1) * capacity
            ].astype(jnp.bfloat16)
    for at in range(0, width, tile):
        cols = slice(at, at + tile)
        out = jnp.dot(hidden_ref[:, :units], wout_a[:, cols], preferred_element_type=jnp.float32)
        out += jnp.dot(hidden_ref[:, units:], wout_b[:, cols], preferred_element_type=jnp.float32)
        for i, ref in enumerate(outs):
            parts = []
            for k in (0, 1) if i % 2 == 0 else (2, 3):
                for s in backs[i // 2]:
                    start = blocks.index((s, k)) * capacity
                    parts.append(out[start : start + capacity])
            ref[:, cols] = jnp.concatenate(parts, axis=0).astype(jnp.bfloat16)


def run_expert(chunks, backs, ahead, held, capacity, final, me, pieces, weights):
    width = pieces[0].shape[1]
    units = weights[2].shape[0]
    rows = sum(piece.shape[0] for piece in pieces)
    places = rows // capacity + (sum(len(earlier) for earlier in ahead) if final else 0)
    hid = jax.ShapeDtypeStruct((places, capacity, units), jnp.bfloat16)
    outs = [
        jax.ShapeDtypeStruct((2 * len(back) * capacity, width), jnp.bfloat16)
        for back in backs
        for _ in (0, 1)
    ]
    return pl.pallas_call(
        functools.partial(expert_kernel, chunks, backs, ahead, final),
        out_shape=outs + [hid] * 2,
        in_specs=[SMEM] + [VMEM] * (len(pieces) + 4 + len(held)),
        out_specs=[VMEM] * (len(outs) + 2),
        scratch_shapes=[
            pltpu.VMEM((rows, width), jnp.bfloat16),
            pltpu.VMEM((rows, 2 * units), jnp.bfloat16),
        ],
        compiler_params=pltpu.CompilerParams(vmem_limit_bytes=16 * MIB),
        cost_estimate=pl.CostEstimate(flops=1, bytes_accessed=1, transcendentals=0),
    )(me, *pieces, *weights, *held)


def weave_kernel(me_ref, mine_ref, other_ref, out_ref):
    core = me_ref[0] % 2
    out_ref[:, pl.ds(core, 1)] = mine_ref[...][:, None]
    out_ref[:, pl.ds(1 - core, 1)] = other_ref[...][:, None]


def keep_kernel(me_ref, swap_ref, mine_ref, far_ref, out_ref):
    flag = swap_ref[me_ref[0] % swap_ref.shape[0]]
    out_ref[...] = jnp.where(flag == 1, far_ref[...], mine_ref[...])


def mix_kernel(hi_ref, lo_ref, *refs):
    values = [r[...].astype(jnp.float32) for r in refs[:-1]]
    rows = jnp.concatenate(values, axis=0).astype(jnp.bfloat16)
    total = jnp.dot(hi_ref[...], rows, preferred_element_type=jnp.float32)
    total += jnp.dot(lo_ref[...], rows, preferred_element_type=jnp.float32)
    refs[-1][...] = total.astype(jnp.bfloat16)


GATHER = [[0], [1, 3], [2]]
BACKS = [[3], [2], [1], [0]]
GROUPS = [[0, 1], [2]]
PLAN = (
    ("Z", 3, 3), ("L", 0, 0), ("Z", 1, 3), ("W", 1, 1), ("z", 1, 0), ("l", 0, 0), ("z", 3, 3),
    ("X", 0, 0), ("W", 0, 3), ("Z", 2, 3), ("L", 1, 3), ("l", 1, 2), ("X", 1, 2), ("w", 0, 1),
    ("z", 2, 3), ("L", 2, 0), ("w", 1, 2), ("x", 0, 1), ("l", 2, 3), ("X", 2, 1), ("x", 1, 0),
    ("K", 0, 0), ("x", 2, 0), ("K", 1, 0), ("C", 1, 0), ("C", 0, 0), ("H", 0, 1), ("h", 0, 0),
    ("C", 2, 0), ("F", 0, 1), ("c", 1, 2), ("c", 0, 0), ("C", 3, 1), ("A", 0, 2), ("a", 0, 3),
    ("A", 1, 0), ("c", 2, 0), ("a", 1, 1), ("B", 2, 0), ("c", 3, 2), ("A", 2, 0), ("a", 2, 2),
    ("A", 3, 0), ("f", 0, 2), ("b", 2, 1), ("B", 3, 0), ("B", 1, 0), ("b", 3, 2), ("a", 3, 1),
    ("b", 1, 1),
)


def plain_plan(experts):
    steps = [("W", 0), ("W", 1)] + [("Z", s) for s in range(1, experts)] + [("w", 0), ("w", 1)]
    steps += [("z", s) for s in range(1, experts)]
    for s in range(experts):
        steps += [("L", s), ("l", s), ("X", s), ("x", s)]
    steps += [("K", 0), ("H", 0), ("h", 0), ("F", 0), ("f", 0)]
    for s in range(experts):
        steps += [("C", s), ("c", s), ("A", s), ("a", s)]
    steps += [("B", s) for s in range(1, experts)] + [("b", s) for s in range(1, experts)]
    return [(kind, at, 0) for kind, at in steps]


def shards(tokens, route_token, route_expert, route_gate, w_in, w_out, swap_pairs):
    devices = lax.axis_size("ep")
    half_axis = devices // 2
    tok_count, width = tokens.shape
    units = w_out.shape[1]
    rows_dev = route_token.shape[0]
    experts = devices // SLICES
    capacity = min(rows_dev, 3 * rows_dev // (2 * experts))
    places = experts * capacity
    me = lax.axis_index("ep").astype(jnp.int32).reshape(1)
    small = pltpu.CompilerParams(vmem_limit_bytes=16 * MIB)
    tuned = experts == 1 + max(max(chunk) for chunk in GATHER)
    singles = [[s] for s in range(experts)]
    chunks, backs, groups = (GATHER, BACKS, GROUPS) if tuned else (singles, singles, [list(range(experts))])
    plan = PLAN if tuned else plain_plan(experts)

    *bufs, gate_hi, gate_lo = run_route(
        experts, capacity, me, route_expert, route_token, route_gate, tokens
    )
    both_weights = [w_in[0], w_out[0]]
    flying, came, both = {}, {("z", 0): bufs[0]}, {}
    near, away, sums, held, ahead = {}, {}, {}, [], []
    token = me

    def send(key, value, mask_of, mark):
        nonlocal token
        if mark == 3:
            token, value = lax.optimization_barrier((token, value))
        elif mark == 2:
            token = after(token, value)
        elif mark == 1:
            value = after(value, token)
        flying[key] = swap(value, mask_of)

    for kind, s, mark in plan:
        if kind == "W":
            send(("w", s), both_weights[s], lambda i: CORE, mark)
        elif kind == "Z":
            send(("z", s), bufs[s], lambda i: SLICES * s, mark)
        elif kind == "L":
            both[s] = [came["z", e] for e in chunks[s]]
            mine = jnp.concatenate(both[s], axis=0) if len(both[s]) > 1 else both[s][0]
            send(("l", s), mine, lane, mark)
        elif kind == "X":
            both[s] = jnp.concatenate(both[s] + [came["l", s]], axis=0)
            send(("x", s), both[s], cross, mark)
        elif kind == "K":
            group = groups[s]
            pieces = sum([[both[c], came["x", c]] for c in group], [])
            weights = [w_in[0], came["w", 0], w_out[0], came["w", 1]]
            inside = [e for c in group for e in chunks[c]]
            mine = [i for i, back in enumerate(backs) if back[0] in inside]
            final = s == len(groups) - 1
            *outs, hid_a, hid_b = run_expert(
                [chunks[c] for c in group],
                [backs[i] for i in mine],
                ahead if final else [],
                held if final else [],
                capacity,
                final,
                me,
                pieces,
                weights,
            )
            held = held + [hid_a, hid_b]
            ahead = ahead + [[(e, k) for c in group for k in range(4) for e in chunks[c]]]
            for i, index in enumerate(mine):
                near[index], away[index] = outs[2 * i : 2 * i + 2]
        elif kind == "C":
            send(("c", s), away[s], cross, mark)
        elif kind == "A":
            half = near[s].shape[0] // 2
            relay = near[s][half:].astype(jnp.float32) + came["c", s][half:].astype(jnp.float32)
            send(("a", s), relay.astype(jnp.bfloat16), lane, mark)
        elif kind == "B":
            send(("b", s), sums[s], lambda i: SLICES * s, mark)
        elif kind == "H":
            send(("h", 0), hid_b, lambda i: CORE, mark)
        elif kind == "F":
            full = pl.pallas_call(
                weave_kernel,
                out_shape=jax.ShapeDtypeStruct((devices // 2, 2, capacity, units), jnp.bfloat16),
                in_specs=[SMEM, VMEM, VMEM],
                out_specs=VMEM,
                compiler_params=small,
            )(me, hid_a, came["h", 0])
            send(("f", 0), full, lambda i: half_axis, mark)
        else:
            value = flying[kind, s]
            if mark == 3:
                token, value = lax.optimization_barrier((token, value))
            elif mark == 2:
                token = after(token, value)
            elif mark == 1:
                value = after(value, token)
            came[kind, s] = value
            if kind == "a":
                parts = (near[s], came["c", s], came["a", s])
                for i, e in enumerate(backs[s]):
                    rows = slice(i * capacity, (i + 1) * capacity)
                    total = sum(part[rows].astype(jnp.float32) for part in parts)
                    sums[e] = total.astype(jnp.bfloat16)

    saved = pl.pallas_call(
        keep_kernel,
        out_shape=jax.ShapeDtypeStruct(full.shape, full.dtype),
        in_specs=[SMEM, SMEM, VMEM, VMEM],
        out_specs=pl.BlockSpec(),
        compiler_params=small,
    )(me, swap_pairs, full, came["f", 0])
    finals = after([sums[0]] + [came["b", s] for s in range(1, experts)], token)
    tile = column_tile(width)
    moving = lambda rows: pl.BlockSpec((rows, tile), lambda i: (0, i))
    fixed = pl.BlockSpec((tok_count, places), lambda i: (0, 0))
    mixed = pl.pallas_call(
        mix_kernel,
        out_shape=jax.ShapeDtypeStruct((tok_count, width), jnp.bfloat16),
        grid=(width // tile,),
        in_specs=[fixed] * 2 + [moving(capacity)] * experts,
        out_specs=moving(tok_count),
        compiler_params=small,
    )(gate_hi, gate_lo, *finals)
    return (mixed, saved.reshape(1, devices * capacity, units))


def solution(mesh):
    return jax.shard_map(
        shards,
        mesh=mesh,
        in_specs=(
            P(("rep", "ep"), None),
            P(("rep", "ep")),
            P(("rep", "ep"), None),
            P(("rep", "ep")),
            P("ep", None, None),
            P("ep", None, None),
            P(),
        ),
        out_specs=(P(("rep", "ep"), None), P(("rep", "ep"), None, None)),
        check_vma=False,
    )
```

```python
import functools

import jax
import jax.numpy as jnp
from jax import lax
from jax.experimental import pallas as pl
from jax.experimental.pallas import tpu as pltpu
from jax.sharding import PartitionSpec as P

SLICES = 8
CORE, FIRST, SECOND = 1, 2, 4
CHIPS = SLICES // 2
VMEM = pl.BlockSpec(memory_space=pltpu.VMEM)
SMEM = pl.BlockSpec(memory_space=pltpu.SMEM)
ANY = pl.BlockSpec(memory_space=pl.ANY)
MIB = 1024 * 1024


def swap(value, mask_of):
    count = lax.axis_size("ep")
    return lax.ppermute(value, "ep", [(i, i ^ mask_of(i)) for i in range(count)])


def after(value, others):
    return lax.optimization_barrier((value, others))[0]


def lane(i):
    return FIRST if i & CORE == 0 else SECOND


def cross(i):
    return SECOND if i & CORE == 0 else FIRST


def column_tile(width):
    return next(t for t in (1792, 512, 256, 128, width) if width % t == 0)


def route_kernel(experts, capacity, me_ref, expert_hbm, token_hbm, gate_hbm, tok_hbm, *refs):
    bufs, (hi_ref, lo_ref) = refs[:experts], refs[experts : experts + 2]
    expert_ref, token_ref, gate_ref, tok_ref, sems = refs[experts + 2 :]
    rows = expert_ref.shape[1]
    tok_count, width = tok_ref.shape
    places = experts * capacity
    tile = column_tile(width)
    tiles = width // tile
    small = [
        pltpu.make_async_copy(source, target, sems.at[i])
        for i, (source, target) in enumerate(
            ((expert_hbm, expert_ref), (token_hbm, token_ref), (gate_hbm, gate_ref))
        )
    ]
    large = [
        pltpu.make_async_copy(
            tok_hbm.at[:, pl.ds(k * tile, tile)], tok_ref.at[:, pl.ds(k * tile, tile)], sems.at[3 + k]
        )
        for k in range(tiles)
    ]
    for copy in small + large:
        copy.start()
    for copy in small:
        copy.wait()
    relative = expert_ref[...] ^ (me_ref[0] // SLICES)
    ranks = -(-experts // 8) * 8
    hits = (lax.broadcasted_iota(jnp.int32, (ranks, rows), 0) == relative).astype(jnp.float32)
    earlier = lax.broadcasted_iota(jnp.int32, (rows, rows), 0) < lax.broadcasted_iota(
        jnp.int32, (rows, rows), 1
    )
    before = jnp.dot(
        hits.astype(jnp.bfloat16),
        earlier.astype(jnp.float32).astype(jnp.bfloat16),
        preferred_element_type=jnp.float32,
    )
    slot = jnp.sum(hits * before, axis=0, keepdims=True).astype(jnp.int32)
    target = relative * capacity + slot
    place_hot = lax.broadcasted_iota(jnp.int32, (places, rows), 0) == target
    place_hot = place_hot.astype(jnp.float32).astype(jnp.bfloat16)
    token_hot = lax.broadcasted_iota(jnp.int32, (tok_count, rows), 0) == token_ref[...]
    token_hot = token_hot.astype(jnp.float32)
    contract = (((1,), (1,)), ((), ()))
    pick = lax.dot_general(
        place_hot, token_hot.astype(jnp.bfloat16), contract, preferred_element_type=jnp.float32
    ).astype(jnp.bfloat16)
    for k in range(tiles):
        cols = pl.ds(k * tile, tile)
        large[k].wait()
        picked = jnp.dot(pick, tok_ref[:, cols], preferred_element_type=jnp.float32)
        for s in range(experts):
            bufs[s][:, cols] = picked[s * capacity : (s + 1) * capacity].astype(jnp.bfloat16)
    gate = gate_ref[...]
    gate_hi = gate.astype(jnp.bfloat16).astype(jnp.float32)
    for part, ref in ((gate_hi, hi_ref), (gate - gate_hi, lo_ref)):
        ref[...] = lax.dot_general(
            (token_hot * part).astype(jnp.bfloat16),
            place_hot,
            contract,
            preferred_element_type=jnp.float32,
        ).astype(jnp.bfloat16)


def run_route(experts, capacity, me, route_expert, route_token, route_gate, tokens):
    tok_count, width = tokens.shape
    rows = route_token.shape[0]
    block = jax.ShapeDtypeStruct((capacity, width), jnp.bfloat16)
    mix = jax.ShapeDtypeStruct((tok_count, experts * capacity), jnp.bfloat16)
    return pl.pallas_call(
        functools.partial(route_kernel, experts, capacity),
        out_shape=[block] * experts + [mix] * 2,
        in_specs=[SMEM] + [ANY] * 4,
        out_specs=[VMEM] * (experts + 2),
        scratch_shapes=[
            pltpu.VMEM((1, rows), jnp.int32),
            pltpu.VMEM((1, rows), jnp.int32),
            pltpu.VMEM((1, rows), jnp.float32),
            pltpu.VMEM((tok_count, width), jnp.bfloat16),
            pltpu.SemaphoreType.DMA((3 + width // column_tile(width),)),
        ],
        compiler_params=pltpu.CompilerParams(vmem_limit_bytes=60 * MIB),
    )(
        me,
        route_expert.reshape(1, rows),
        route_token.reshape(1, rows),
        route_gate.reshape(1, rows),
        tokens,
    )


def expert_kernel(chunks, backs, ahead, final, me_ref, *refs):
    count = 2 * len(chunks)
    pieces, (win_a, win_b, wout_a, wout_b) = refs[:count], refs[count : count + 4]
    held, refs = refs[count + 4 : count + 4 + 2 * len(ahead)], refs[count + 4 + 2 * len(ahead) :]
    outs, hids = refs[: 2 * len(backs)], refs[2 * len(backs) : -2]
    rows_ref, hidden_ref = refs[-2:]
    units, width = wout_a.shape
    capacity = hids[0].shape[1]
    tile = column_tile(width)
    at = 0
    for piece in pieces:
        rows_ref[at : at + piece.shape[0]] = piece[...]
        at += piece.shape[0]
    me = me_ref[0]
    layer, chip, core = me // SLICES, (me % SLICES) // 2, me % 2
    lane_mask = (FIRST + core * (SECOND - FIRST)) // 2
    cross_mask = (SECOND - core * (SECOND - FIRST)) // 2
    masks = (0, lane_mask, cross_mask, lane_mask ^ cross_mask)
    blocks = [(s, k) for chunk in chunks for k in range(4) for s in chunk]

    def spot(s, k):
        return (layer ^ s) * CHIPS + (chip ^ masks[k])

    for e, earlier in enumerate(ahead):
        for half in (0, 1):
            for i, (s, k) in enumerate(earlier):
                hids[half][spot(s, k)] = held[2 * e + half][i]
    for half, (win, hid) in enumerate(zip((win_a, win_b), hids)):
        total = jnp.dot(rows_ref[...], win[...], preferred_element_type=jnp.float32)
        gate, up = total[:, :units], total[:, units:]
        value = (gate / (1.0 + jnp.exp(-gate)) * up).astype(jnp.bfloat16)
        hidden_ref[:, units * half : units * (half + 1)] = value
        value = value.astype(jnp.float32)
        for i, (s, k) in enumerate(blocks):
            hid[spot(s, k) if final else i] = value[
                i * capacity : (i + 1) * capacity
            ].astype(jnp.bfloat16)
    for at in range(0, width, tile):
        cols = slice(at, at + tile)
        out = jnp.dot(hidden_ref[:, :units], wout_a[:, cols], preferred_element_type=jnp.float32)
        out += jnp.dot(hidden_ref[:, units:], wout_b[:, cols], preferred_element_type=jnp.float32)
        for i, ref in enumerate(outs):
            parts = []
            for k in (0, 1) if i % 2 == 0 else (2, 3):
                for s in backs[i // 2]:
                    start = blocks.index((s, k)) * capacity
                    parts.append(out[start : start + capacity])
            ref[:, cols] = jnp.concatenate(parts, axis=0).astype(jnp.bfloat16)


def run_expert(chunks, backs, ahead, held, capacity, final, me, pieces, weights):
    width = pieces[0].shape[1]
    units = weights[2].shape[0]
    rows = sum(piece.shape[0] for piece in pieces)
    places = rows // capacity + (sum(len(earlier) for earlier in ahead) if final else 0)
    hid = jax.ShapeDtypeStruct((places, capacity, units), jnp.bfloat16)
    outs = [
        jax.ShapeDtypeStruct((2 * len(back) * capacity, width), jnp.bfloat16)
        for back in backs
        for _ in (0, 1)
    ]
    return pl.pallas_call(
        functools.partial(expert_kernel, chunks, backs, ahead, final),
        out_shape=outs + [hid] * 2,
        in_specs=[SMEM] + [VMEM] * (len(pieces) + 4 + len(held)),
        out_specs=[VMEM] * (len(outs) + 2),
        scratch_shapes=[
            pltpu.VMEM((rows, width), jnp.bfloat16),
            pltpu.VMEM((rows, 2 * units), jnp.bfloat16),
        ],
        compiler_params=pltpu.CompilerParams(vmem_limit_bytes=16 * MIB),
        cost_estimate=pl.CostEstimate(flops=1, bytes_accessed=1, transcendentals=0),
    )(me, *pieces, *weights, *held)


def weave_kernel(me_ref, mine_ref, other_ref, out_ref):
    core = me_ref[0] % 2
    out_ref[:, pl.ds(core, 1)] = mine_ref[...][:, None]
    out_ref[:, pl.ds(1 - core, 1)] = other_ref[...][:, None]


def keep_kernel(me_ref, swap_ref, mine_ref, far_ref, out_ref):
    flag = swap_ref[me_ref[0] % swap_ref.shape[0]]
    out_ref[...] = jnp.where(flag == 1, far_ref[...], mine_ref[...])


def mix_kernel(hi_ref, lo_ref, *refs):
    values, out, (stage_ref, sems) = refs[:-3], refs[-3], refs[-2:]
    width = stage_ref.shape[1]
    tile = column_tile(width)
    copies = []
    for k in range(width // tile):
        cols = pl.ds(k * tile, tile)
        rows = jnp.concatenate([r[:, cols].astype(jnp.float32) for r in values], axis=0)
        rows = rows.astype(jnp.bfloat16)
        total = jnp.dot(hi_ref[...], rows, preferred_element_type=jnp.float32)
        total += jnp.dot(lo_ref[...], rows, preferred_element_type=jnp.float32)
        stage_ref[:, cols] = total.astype(jnp.bfloat16)
        copy = pltpu.make_async_copy(stage_ref.at[:, cols], out.at[:, cols], sems.at[k])
        copy.start()
        copies.append(copy)
    for copy in copies:
        copy.wait()


GATHER = [[0], [1, 3], [2]]
BACKS = [[3], [2], [1], [0]]
GROUPS = [[0, 1], [2]]
PLAN = (
    ("Z", 3, 3), ("L", 0, 0), ("Z", 1, 0), ("W", 1, 1), ("z", 1, 0), ("l", 0, 0), ("z", 3, 3),
    ("X", 0, 0), ("W", 0, 2), ("Z", 2, 3), ("L", 1, 3), ("l", 1, 2), ("X", 1, 2), ("w", 0, 1),
    ("z", 2, 3), ("L", 2, 0), ("w", 1, 0), ("x", 0, 1), ("l", 2, 3), ("X", 2, 1), ("x", 1, 0),
    ("K", 0, 0), ("x", 2, 0), ("K", 1, 0), ("C", 2, 0), ("C", 0, 0), ("C", 1, 0), ("H", 0, 1),
    ("h", 0, 0), ("F", 0, 1), ("c", 0, 2), ("A", 0, 2), ("c", 1, 1), ("A", 1, 2), ("a", 0, 1),
    ("B", 3, 2), ("c", 2, 1), ("A", 2, 0), ("a", 1, 0), ("B", 2, 0), ("f", 0, 1), ("C", 3, 1),
    ("a", 2, 0), ("B", 1, 0), ("c", 3, 0), ("A", 3, 0), ("a", 3, 0), ("b", 3, 0), ("b", 2, 1),
    ("b", 1, 0),
)


def plain_plan(experts):
    steps = [("W", 0), ("W", 1)] + [("Z", s) for s in range(1, experts)] + [("w", 0), ("w", 1)]
    steps += [("z", s) for s in range(1, experts)]
    for s in range(experts):
        steps += [("L", s), ("l", s), ("X", s), ("x", s)]
    steps += [("K", 0), ("H", 0), ("h", 0), ("F", 0), ("f", 0)]
    for s in range(experts):
        steps += [("C", s), ("c", s), ("A", s), ("a", s)]
    steps += [("B", s) for s in range(1, experts)] + [("b", s) for s in range(1, experts)]
    return [(kind, at, 0) for kind, at in steps]


def shards(tokens, route_token, route_expert, route_gate, w_in, w_out, swap_pairs):
    devices = lax.axis_size("ep")
    half_axis = devices // 2
    tok_count, width = tokens.shape
    units = w_out.shape[1]
    rows_dev = route_token.shape[0]
    experts = devices // SLICES
    capacity = min(rows_dev, 3 * rows_dev // (2 * experts))
    places = experts * capacity
    me = lax.axis_index("ep").astype(jnp.int32).reshape(1)
    small = pltpu.CompilerParams(vmem_limit_bytes=16 * MIB)
    tuned = experts == 1 + max(max(chunk) for chunk in GATHER)
    singles = [[s] for s in range(experts)]
    chunks, backs, groups = (GATHER, BACKS, GROUPS) if tuned else (singles, singles, [list(range(experts))])
    plan = PLAN if tuned else plain_plan(experts)

    *bufs, gate_hi, gate_lo = run_route(
        experts, capacity, me, route_expert, route_token, route_gate, tokens
    )
    both_weights = [w_in[0], w_out[0]]
    flying, came, both = {}, {("z", 0): bufs[0]}, {}
    near, away, sums, held, ahead = {}, {}, {}, [], []
    token = me

    def send(key, value, mask_of, mark):
        nonlocal token
        if mark == 3:
            token, value = lax.optimization_barrier((token, value))
        elif mark == 2:
            token = after(token, value)
        elif mark == 1:
            value = after(value, token)
        flying[key] = swap(value, mask_of)

    for kind, s, mark in plan:
        if kind == "W":
            send(("w", s), both_weights[s], lambda i: CORE, mark)
        elif kind == "Z":
            send(("z", s), bufs[s], lambda i: SLICES * s, mark)
        elif kind == "L":
            both[s] = [came["z", e] for e in chunks[s]]
            mine = jnp.concatenate(both[s], axis=0) if len(both[s]) > 1 else both[s][0]
            send(("l", s), mine, lane, mark)
        elif kind == "X":
            both[s] = jnp.concatenate(both[s] + [came["l", s]], axis=0)
            send(("x", s), both[s], cross, mark)
        elif kind == "K":
            group = groups[s]
            pieces = sum([[both[c], came["x", c]] for c in group], [])
            weights = [w_in[0], came["w", 0], w_out[0], came["w", 1]]
            inside = [e for c in group for e in chunks[c]]
            mine = [i for i, back in enumerate(backs) if back[0] in inside]
            final = s == len(groups) - 1
            *outs, hid_a, hid_b = run_expert(
                [chunks[c] for c in group],
                [backs[i] for i in mine],
                ahead if final else [],
                held if final else [],
                capacity,
                final,
                me,
                pieces,
                weights,
            )
            held = held + [hid_a, hid_b]
            ahead = ahead + [[(e, k) for c in group for k in range(4) for e in chunks[c]]]
            for i, index in enumerate(mine):
                near[index], away[index] = outs[2 * i : 2 * i + 2]
        elif kind == "C":
            send(("c", s), away[s], cross, mark)
        elif kind == "A":
            half = near[s].shape[0] // 2
            relay = near[s][half:].astype(jnp.float32) + came["c", s][half:].astype(jnp.float32)
            send(("a", s), relay.astype(jnp.bfloat16), lane, mark)
        elif kind == "B":
            send(("b", s), sums[s], lambda i: SLICES * s, mark)
        elif kind == "H":
            send(("h", 0), hid_b, lambda i: CORE, mark)
        elif kind == "F":
            full = pl.pallas_call(
                weave_kernel,
                out_shape=jax.ShapeDtypeStruct((devices // 2, 2, capacity, units), jnp.bfloat16),
                in_specs=[SMEM, VMEM, VMEM],
                out_specs=VMEM,
                compiler_params=small,
            )(me, hid_a, came["h", 0])
            send(("f", 0), full, lambda i: half_axis, mark)
        else:
            value = flying[kind, s]
            if mark == 3:
                token, value = lax.optimization_barrier((token, value))
            elif mark == 2:
                token = after(token, value)
            elif mark == 1:
                value = after(value, token)
            came[kind, s] = value
            if kind == "a":
                parts = (near[s], came["c", s], came["a", s])
                for i, e in enumerate(backs[s]):
                    rows = slice(i * capacity, (i + 1) * capacity)
                    total = sum(part[rows].astype(jnp.float32) for part in parts)
                    sums[e] = total.astype(jnp.bfloat16)

    saved = pl.pallas_call(
        keep_kernel,
        out_shape=jax.ShapeDtypeStruct(full.shape, full.dtype),
        in_specs=[SMEM, SMEM, VMEM, VMEM],
        out_specs=pl.BlockSpec(),
        compiler_params=small,
    )(me, swap_pairs, full, came["f", 0])
    finals = after([sums[0]] + [came["b", s] for s in range(1, experts)], token)
    mixed = pl.pallas_call(
        mix_kernel,
        out_shape=jax.ShapeDtypeStruct((tok_count, width), jnp.bfloat16),
        in_specs=[VMEM] * (2 + experts),
        out_specs=ANY,
        scratch_shapes=[
            pltpu.VMEM((tok_count, width), jnp.bfloat16),
            pltpu.SemaphoreType.DMA((width // column_tile(width),)),
        ],
        compiler_params=small,
    )(gate_hi, gate_lo, *finals)
    return (mixed, saved.reshape(1, devices * capacity, units))


def solution(mesh):
    return jax.shard_map(
        shards,
        mesh=mesh,
        in_specs=(
            P(("rep", "ep"), None),
            P(("rep", "ep")),
            P(("rep", "ep"), None),
            P(("rep", "ep")),
            P("ep", None, None),
            P("ep", None, None),
            P(),
        ),
        out_specs=(P(("rep", "ep"), None), P(("rep", "ep"), None, None)),
        check_vma=False,
    )
```

```python
import functools

import jax
import jax.numpy as jnp
from jax import lax
from jax.experimental import pallas as pl
from jax.experimental.pallas import tpu as pltpu
from jax.sharding import PartitionSpec as P

SLICES = 8
CORE, FIRST, SECOND = 1, 2, 4
CHIPS = SLICES // 2
VMEM = pl.BlockSpec(memory_space=pltpu.VMEM)
SMEM = pl.BlockSpec(memory_space=pltpu.SMEM)
ANY = pl.BlockSpec(memory_space=pl.ANY)
MIB = 1024 * 1024


def swap(value, mask_of):
    count = lax.axis_size("ep")
    return lax.ppermute(value, "ep", [(i, i ^ mask_of(i)) for i in range(count)])


def after(value, others):
    return lax.optimization_barrier((value, others))[0]


def lane(i):
    return FIRST if i & CORE == 0 else SECOND


def cross(i):
    return SECOND if i & CORE == 0 else FIRST


def column_tile(width):
    return next(t for t in (1792, 512, 256, 128, width) if width % t == 0)


def route_kernel(experts, capacity, me_ref, expert_hbm, token_hbm, gate_hbm, tok_hbm, *refs):
    bufs, (hi_ref, lo_ref) = refs[:experts], refs[experts : experts + 2]
    expert_ref, token_ref, gate_ref, tok_ref, sems = refs[experts + 2 :]
    rows = expert_ref.shape[1]
    tok_count, width = tok_ref.shape
    places = experts * capacity
    tile = column_tile(width)
    tiles = width // tile
    small = [
        pltpu.make_async_copy(source, target, sems.at[i])
        for i, (source, target) in enumerate(
            ((expert_hbm, expert_ref), (token_hbm, token_ref), (gate_hbm, gate_ref))
        )
    ]
    large = [
        pltpu.make_async_copy(
            tok_hbm.at[:, pl.ds(k * tile, tile)], tok_ref.at[:, pl.ds(k * tile, tile)], sems.at[3 + k]
        )
        for k in range(tiles)
    ]
    for copy in small + large:
        copy.start()
    for copy in small:
        copy.wait()
    relative = expert_ref[...] ^ (me_ref[0] // SLICES)
    ranks = -(-experts // 8) * 8
    hits = (lax.broadcasted_iota(jnp.int32, (ranks, rows), 0) == relative).astype(jnp.float32)
    earlier = lax.broadcasted_iota(jnp.int32, (rows, rows), 0) < lax.broadcasted_iota(
        jnp.int32, (rows, rows), 1
    )
    before = jnp.dot(
        hits.astype(jnp.bfloat16),
        earlier.astype(jnp.float32).astype(jnp.bfloat16),
        preferred_element_type=jnp.float32,
    )
    slot = jnp.sum(hits * before, axis=0, keepdims=True).astype(jnp.int32)
    target = relative * capacity + slot
    place_hot = lax.broadcasted_iota(jnp.int32, (places, rows), 0) == target
    place_hot = place_hot.astype(jnp.float32).astype(jnp.bfloat16)
    token_hot = lax.broadcasted_iota(jnp.int32, (tok_count, rows), 0) == token_ref[...]
    token_hot = token_hot.astype(jnp.float32)
    contract = (((1,), (1,)), ((), ()))
    pick = lax.dot_general(
        place_hot, token_hot.astype(jnp.bfloat16), contract, preferred_element_type=jnp.float32
    ).astype(jnp.bfloat16)
    for k in range(tiles):
        cols = pl.ds(k * tile, tile)
        large[k].wait()
        picked = jnp.dot(pick, tok_ref[:, cols], preferred_element_type=jnp.float32)
        for s in range(experts):
            bufs[s][:, cols] = picked[s * capacity : (s + 1) * capacity].astype(jnp.bfloat16)
    gate = gate_ref[...]
    gate_hi = gate.astype(jnp.bfloat16).astype(jnp.float32)
    for part, ref in ((gate_hi, hi_ref), (gate - gate_hi, lo_ref)):
        ref[...] = lax.dot_general(
            (token_hot * part).astype(jnp.bfloat16),
            place_hot,
            contract,
            preferred_element_type=jnp.float32,
        ).astype(jnp.bfloat16)


def run_route(experts, capacity, me, route_expert, route_token, route_gate, tokens):
    tok_count, width = tokens.shape
    rows = route_token.shape[0]
    block = jax.ShapeDtypeStruct((capacity, width), jnp.bfloat16)
    mix = jax.ShapeDtypeStruct((tok_count, experts * capacity), jnp.bfloat16)
    return pl.pallas_call(
        functools.partial(route_kernel, experts, capacity),
        out_shape=[block] * experts + [mix] * 2,
        in_specs=[SMEM] + [ANY] * 4,
        out_specs=[VMEM] * (experts + 2),
        scratch_shapes=[
            pltpu.VMEM((1, rows), jnp.int32),
            pltpu.VMEM((1, rows), jnp.int32),
            pltpu.VMEM((1, rows), jnp.float32),
            pltpu.VMEM((tok_count, width), jnp.bfloat16),
            pltpu.SemaphoreType.DMA((3 + width // column_tile(width),)),
        ],
        compiler_params=pltpu.CompilerParams(vmem_limit_bytes=60 * MIB),
    )(
        me,
        route_expert.reshape(1, rows),
        route_token.reshape(1, rows),
        route_gate.reshape(1, rows),
        tokens,
    )


def expert_kernel(chunks, backs, ahead, final, me_ref, *refs):
    count = 2 * len(chunks)
    pieces, (win_a, win_b, wout_a, wout_b) = refs[:count], refs[count : count + 4]
    held, refs = refs[count + 4 : count + 4 + 2 * len(ahead)], refs[count + 4 + 2 * len(ahead) :]
    outs, hids = refs[: 2 * len(backs)], refs[2 * len(backs) : -2]
    rows_ref, hidden_ref = refs[-2:]
    units, width = wout_a.shape
    capacity = hids[0].shape[1]
    tile = column_tile(width)
    at = 0
    for piece in pieces:
        rows_ref[at : at + piece.shape[0]] = piece[...]
        at += piece.shape[0]
    me = me_ref[0]
    layer, chip, core = me // SLICES, (me % SLICES) // 2, me % 2
    lane_mask = (FIRST + core * (SECOND - FIRST)) // 2
    cross_mask = (SECOND - core * (SECOND - FIRST)) // 2
    masks = (0, lane_mask, cross_mask, lane_mask ^ cross_mask)
    blocks = [(s, k) for chunk in chunks for k in range(4) for s in chunk]

    def spot(s, k):
        return (layer ^ s) * CHIPS + (chip ^ masks[k])

    for e, earlier in enumerate(ahead):
        for half in (0, 1):
            for i, (s, k) in enumerate(earlier):
                hids[half][spot(s, k)] = held[2 * e + half][i]
    for half, (win, hid) in enumerate(zip((win_a, win_b), hids)):
        total = jnp.dot(rows_ref[...], win[...], preferred_element_type=jnp.float32)
        gate, up = total[:, :units], total[:, units:]
        value = (gate / (1.0 + jnp.exp(-gate)) * up).astype(jnp.bfloat16)
        hidden_ref[:, units * half : units * (half + 1)] = value
        value = value.astype(jnp.float32)
        for i, (s, k) in enumerate(blocks):
            hid[spot(s, k) if final else i] = value[
                i * capacity : (i + 1) * capacity
            ].astype(jnp.bfloat16)
    for at in range(0, width, tile):
        cols = slice(at, at + tile)
        out = jnp.dot(hidden_ref[:, :units], wout_a[:, cols], preferred_element_type=jnp.float32)
        out += jnp.dot(hidden_ref[:, units:], wout_b[:, cols], preferred_element_type=jnp.float32)
        for i, ref in enumerate(outs):
            parts = []
            for k in (0, 1) if i % 2 == 0 else (2, 3):
                for s in backs[i // 2]:
                    start = blocks.index((s, k)) * capacity
                    parts.append(out[start : start + capacity])
            ref[:, cols] = jnp.concatenate(parts, axis=0).astype(jnp.bfloat16)


def run_expert(chunks, backs, ahead, held, capacity, final, me, pieces, weights):
    width = pieces[0].shape[1]
    units = weights[2].shape[0]
    rows = sum(piece.shape[0] for piece in pieces)
    places = rows // capacity + (sum(len(earlier) for earlier in ahead) if final else 0)
    hid = jax.ShapeDtypeStruct((places, capacity, units), jnp.bfloat16)
    outs = [
        jax.ShapeDtypeStruct((2 * len(back) * capacity, width), jnp.bfloat16)
        for back in backs
        for _ in (0, 1)
    ]
    return pl.pallas_call(
        functools.partial(expert_kernel, chunks, backs, ahead, final),
        out_shape=outs + [hid] * 2,
        in_specs=[SMEM] + [VMEM] * (len(pieces) + 4 + len(held)),
        out_specs=[VMEM] * (len(outs) + 2),
        scratch_shapes=[
            pltpu.VMEM((rows, width), jnp.bfloat16),
            pltpu.VMEM((rows, 2 * units), jnp.bfloat16),
        ],
        compiler_params=pltpu.CompilerParams(vmem_limit_bytes=16 * MIB),
        cost_estimate=pl.CostEstimate(flops=1, bytes_accessed=1, transcendentals=0),
    )(me, *pieces, *weights, *held)


def weave_kernel(me_ref, mine_ref, other_ref, out_ref):
    core = me_ref[0] % 2
    out_ref[:, pl.ds(core, 1)] = mine_ref[...][:, None]
    out_ref[:, pl.ds(1 - core, 1)] = other_ref[...][:, None]


def keep_kernel(me_ref, swap_ref, mine_ref, far_ref, out_ref):
    flag = swap_ref[me_ref[0] % swap_ref.shape[0]]
    out_ref[...] = jnp.where(flag == 1, far_ref[...], mine_ref[...])


def mix_kernel(hi_ref, lo_ref, *refs):
    values, out, (stage_ref, sems) = refs[:-3], refs[-3], refs[-2:]
    width = stage_ref.shape[1]
    tile = column_tile(width)
    copies = []
    for k in range(width // tile):
        cols = pl.ds(k * tile, tile)
        rows = jnp.concatenate([r[:, cols].astype(jnp.float32) for r in values], axis=0)
        rows = rows.astype(jnp.bfloat16)
        total = jnp.dot(hi_ref[...], rows, preferred_element_type=jnp.float32)
        total += jnp.dot(lo_ref[...], rows, preferred_element_type=jnp.float32)
        stage_ref[:, cols] = total.astype(jnp.bfloat16)
        copy = pltpu.make_async_copy(stage_ref.at[:, cols], out.at[:, cols], sems.at[k])
        copy.start()
        copies.append(copy)
    for copy in copies:
        copy.wait()


GATHER = [[0], [1, 3], [2]]
BACKS = [[3], [2], [1], [0]]
GROUPS = [[0, 1], [2]]
PLAN = (
    ("Z", 3, 3), ("L", 0, 0), ("Z", 1, 0), ("W", 1, 1), ("l", 0, 0), ("X", 0, 0), ("z", 3, 3),
    ("Z", 2, 3), ("z", 1, 1), ("W", 0, 2), ("L", 1, 3), ("l", 1, 2), ("X", 1, 2), ("w", 0, 1),
    ("z", 2, 3), ("L", 2, 0), ("w", 1, 0), ("x", 0, 1), ("l", 2, 3), ("X", 2, 1), ("x", 1, 0),
    ("K", 0, 0), ("x", 2, 0), ("K", 1, 0), ("C", 2, 0), ("C", 0, 0), ("C", 1, 0), ("H", 0, 1),
    ("h", 0, 0), ("F", 0, 1), ("c", 0, 2), ("A", 0, 2), ("c", 1, 1), ("A", 1, 2), ("a", 0, 1),
    ("B", 3, 2), ("C", 3, 1), ("c", 2, 1), ("A", 2, 0), ("a", 1, 0), ("B", 2, 0), ("f", 0, 1),
    ("a", 2, 0), ("B", 1, 0), ("c", 3, 0), ("A", 3, 0), ("b", 3, 3), ("b", 2, 3), ("b", 1, 3),
    ("a", 3, 1),
)


def plain_plan(experts):
    steps = [("W", 0), ("W", 1)] + [("Z", s) for s in range(1, experts)] + [("w", 0), ("w", 1)]
    steps += [("z", s) for s in range(1, experts)]
    for s in range(experts):
        steps += [("L", s), ("l", s), ("X", s), ("x", s)]
    steps += [("K", 0), ("H", 0), ("h", 0), ("F", 0), ("f", 0)]
    for s in range(experts):
        steps += [("C", s), ("c", s), ("A", s), ("a", s)]
    steps += [("B", s) for s in range(1, experts)] + [("b", s) for s in range(1, experts)]
    return [(kind, at, 0) for kind, at in steps]


def shards(tokens, route_token, route_expert, route_gate, w_in, w_out, swap_pairs):
    devices = lax.axis_size("ep")
    half_axis = devices // 2
    tok_count, width = tokens.shape
    units = w_out.shape[1]
    rows_dev = route_token.shape[0]
    experts = devices // SLICES
    capacity = min(rows_dev, 3 * rows_dev // (2 * experts))
    places = experts * capacity
    me = lax.axis_index("ep").astype(jnp.int32).reshape(1)
    small = pltpu.CompilerParams(vmem_limit_bytes=16 * MIB)
    tuned = experts == 1 + max(max(chunk) for chunk in GATHER)
    singles = [[s] for s in range(experts)]
    chunks, backs, groups = (GATHER, BACKS, GROUPS) if tuned else (singles, singles, [list(range(experts))])
    plan = PLAN if tuned else plain_plan(experts)

    *bufs, gate_hi, gate_lo = run_route(
        experts, capacity, me, route_expert, route_token, route_gate, tokens
    )
    both_weights = [w_in[0], w_out[0]]
    flying, came, both = {}, {("z", 0): bufs[0]}, {}
    near, away, sums, held, ahead = {}, {}, {}, [], []
    token = me

    def send(key, value, mask_of, mark):
        nonlocal token
        if mark == 3:
            token, value = lax.optimization_barrier((token, value))
        elif mark == 2:
            token = after(token, value)
        elif mark == 1:
            value = after(value, token)
        flying[key] = swap(value, mask_of)

    for kind, s, mark in plan:
        if kind == "W":
            send(("w", s), both_weights[s], lambda i: CORE, mark)
        elif kind == "Z":
            send(("z", s), bufs[s], lambda i: SLICES * s, mark)
        elif kind == "L":
            both[s] = [came["z", e] for e in chunks[s]]
            mine = jnp.concatenate(both[s], axis=0) if len(both[s]) > 1 else both[s][0]
            send(("l", s), mine, lane, mark)
        elif kind == "X":
            both[s] = jnp.concatenate(both[s] + [came["l", s]], axis=0)
            send(("x", s), both[s], cross, mark)
        elif kind == "K":
            group = groups[s]
            pieces = sum([[both[c], came["x", c]] for c in group], [])
            weights = [w_in[0], came["w", 0], w_out[0], came["w", 1]]
            inside = [e for c in group for e in chunks[c]]
            mine = [i for i, back in enumerate(backs) if back[0] in inside]
            final = s == len(groups) - 1
            *outs, hid_a, hid_b = run_expert(
                [chunks[c] for c in group],
                [backs[i] for i in mine],
                ahead if final else [],
                held if final else [],
                capacity,
                final,
                me,
                pieces,
                weights,
            )
            held = held + [hid_a, hid_b]
            ahead = ahead + [[(e, k) for c in group for k in range(4) for e in chunks[c]]]
            for i, index in enumerate(mine):
                near[index], away[index] = outs[2 * i : 2 * i + 2]
        elif kind == "C":
            send(("c", s), away[s], cross, mark)
        elif kind == "A":
            half = near[s].shape[0] // 2
            relay = near[s][half:].astype(jnp.float32) + came["c", s][half:].astype(jnp.float32)
            send(("a", s), relay.astype(jnp.bfloat16), lane, mark)
        elif kind == "B":
            send(("b", s), sums[s], lambda i: SLICES * s, mark)
        elif kind == "H":
            send(("h", 0), hid_b, lambda i: CORE, mark)
        elif kind == "F":
            full = pl.pallas_call(
                weave_kernel,
                out_shape=jax.ShapeDtypeStruct((devices // 2, 2, capacity, units), jnp.bfloat16),
                in_specs=[SMEM, VMEM, VMEM],
                out_specs=VMEM,
                compiler_params=small,
            )(me, hid_a, came["h", 0])
            send(("f", 0), full, lambda i: half_axis, mark)
        else:
            value = flying[kind, s]
            if mark == 3:
                token, value = lax.optimization_barrier((token, value))
            elif mark == 2:
                token = after(token, value)
            elif mark == 1:
                value = after(value, token)
            came[kind, s] = value
            if kind == "a":
                parts = (near[s], came["c", s], came["a", s])
                for i, e in enumerate(backs[s]):
                    rows = slice(i * capacity, (i + 1) * capacity)
                    total = sum(part[rows].astype(jnp.float32) for part in parts)
                    sums[e] = total.astype(jnp.bfloat16)

    saved = pl.pallas_call(
        keep_kernel,
        out_shape=jax.ShapeDtypeStruct(full.shape, full.dtype),
        in_specs=[SMEM, SMEM, VMEM, VMEM],
        out_specs=pl.BlockSpec(),
        compiler_params=small,
    )(me, swap_pairs, full, came["f", 0])
    finals = after([sums[0]] + [came["b", s] for s in range(1, experts)], token)
    mixed = pl.pallas_call(
        mix_kernel,
        out_shape=jax.ShapeDtypeStruct((tok_count, width), jnp.bfloat16),
        in_specs=[VMEM] * (2 + experts),
        out_specs=ANY,
        scratch_shapes=[
            pltpu.VMEM((tok_count, width), jnp.bfloat16),
            pltpu.SemaphoreType.DMA((width // column_tile(width),)),
        ],
        compiler_params=small,
    )(gate_hi, gate_lo, *finals)
    return (mixed, saved.reshape(1, devices * capacity, units))


def solution(mesh):
    return jax.shard_map(
        shards,
        mesh=mesh,
        in_specs=(
            P(("rep", "ep"), None),
            P(("rep", "ep")),
            P(("rep", "ep"), None),
            P(("rep", "ep")),
            P("ep", None, None),
            P("ep", None, None),
            P(),
        ),
        out_specs=(P(("rep", "ep"), None), P(("rep", "ep"), None, None)),
        check_vma=False,
    )
```

```python
import functools

import jax
import jax.numpy as jnp
from jax import lax
from jax.experimental import pallas as pl
from jax.experimental.pallas import tpu as pltpu
from jax.sharding import PartitionSpec as P

SLICES = 8
CORE, FIRST, SECOND = 1, 2, 4
CHIPS = SLICES // 2
VMEM = pl.BlockSpec(memory_space=pltpu.VMEM)
SMEM = pl.BlockSpec(memory_space=pltpu.SMEM)
ANY = pl.BlockSpec(memory_space=pl.ANY)
MIB = 1024 * 1024


def swap(value, mask_of):
    count = lax.axis_size("ep")
    return lax.ppermute(value, "ep", [(i, i ^ mask_of(i)) for i in range(count)])


def after(value, others):
    return lax.optimization_barrier((value, others))[0]


def lane(i):
    return FIRST if i & CORE == 0 else SECOND


def cross(i):
    return SECOND if i & CORE == 0 else FIRST


def column_tile(width):
    return next(t for t in (1792, 512, 256, 128, width) if width % t == 0)


def route_kernel(experts, capacity, me_ref, expert_hbm, token_hbm, gate_hbm, tok_hbm, *refs):
    bufs, (hi_ref, lo_ref) = refs[:experts], refs[experts : experts + 2]
    expert_ref, token_ref, gate_ref, tok_ref, sems = refs[experts + 2 :]
    rows = expert_ref.shape[1]
    tok_count, width = tok_ref.shape
    places = experts * capacity
    tile = column_tile(width)
    tiles = width // tile
    small = [
        pltpu.make_async_copy(source, target, sems.at[i])
        for i, (source, target) in enumerate(
            ((expert_hbm, expert_ref), (token_hbm, token_ref), (gate_hbm, gate_ref))
        )
    ]
    large = [
        pltpu.make_async_copy(
            tok_hbm.at[:, pl.ds(k * tile, tile)], tok_ref.at[:, pl.ds(k * tile, tile)], sems.at[3 + k]
        )
        for k in range(tiles)
    ]
    for copy in small + large:
        copy.start()
    for copy in small:
        copy.wait()
    relative = expert_ref[...] ^ (me_ref[0] // SLICES)
    ranks = -(-experts // 8) * 8
    hits = (lax.broadcasted_iota(jnp.int32, (ranks, rows), 0) == relative).astype(jnp.float32)
    earlier = lax.broadcasted_iota(jnp.int32, (rows, rows), 0) < lax.broadcasted_iota(
        jnp.int32, (rows, rows), 1
    )
    before = jnp.dot(
        hits.astype(jnp.bfloat16),
        earlier.astype(jnp.float32).astype(jnp.bfloat16),
        preferred_element_type=jnp.float32,
    )
    slot = jnp.sum(hits * before, axis=0, keepdims=True).astype(jnp.int32)
    target = relative * capacity + slot
    place_hot = lax.broadcasted_iota(jnp.int32, (places, rows), 0) == target
    place_hot = place_hot.astype(jnp.float32).astype(jnp.bfloat16)
    token_hot = lax.broadcasted_iota(jnp.int32, (tok_count, rows), 0) == token_ref[...]
    token_hot = token_hot.astype(jnp.float32)
    contract = (((1,), (1,)), ((), ()))
    pick = lax.dot_general(
        place_hot, token_hot.astype(jnp.bfloat16), contract, preferred_element_type=jnp.float32
    ).astype(jnp.bfloat16)
    gate = gate_ref[...]
    gate_hi = gate.astype(jnp.bfloat16).astype(jnp.float32)
    for part, ref in ((gate_hi, hi_ref), (gate - gate_hi, lo_ref)):
        ref[...] = lax.dot_general(
            (token_hot * part).astype(jnp.bfloat16),
            place_hot,
            contract,
            preferred_element_type=jnp.float32,
        ).astype(jnp.bfloat16)
    for k in range(tiles):
        cols = pl.ds(k * tile, tile)
        large[k].wait()
        picked = jnp.dot(pick, tok_ref[:, cols], preferred_element_type=jnp.float32)
        for s in range(experts):
            bufs[s][:, cols] = picked[s * capacity : (s + 1) * capacity].astype(jnp.bfloat16)


def run_route(experts, capacity, me, route_expert, route_token, route_gate, tokens):
    tok_count, width = tokens.shape
    rows = route_token.shape[0]
    block = jax.ShapeDtypeStruct((capacity, width), jnp.bfloat16)
    mix = jax.ShapeDtypeStruct((tok_count, experts * capacity), jnp.bfloat16)
    return pl.pallas_call(
        functools.partial(route_kernel, experts, capacity),
        out_shape=[block] * experts + [mix] * 2,
        in_specs=[SMEM] + [ANY] * 4,
        out_specs=[VMEM] * (experts + 2),
        scratch_shapes=[
            pltpu.VMEM((1, rows), jnp.int32),
            pltpu.VMEM((1, rows), jnp.int32),
            pltpu.VMEM((1, rows), jnp.float32),
            pltpu.VMEM((tok_count, width), jnp.bfloat16),
            pltpu.SemaphoreType.DMA((3 + width // column_tile(width),)),
        ],
        compiler_params=pltpu.CompilerParams(vmem_limit_bytes=60 * MIB),
    )(
        me,
        route_expert.reshape(1, rows),
        route_token.reshape(1, rows),
        route_gate.reshape(1, rows),
        tokens,
    )


def expert_kernel(chunks, backs, ahead, final, me_ref, *refs):
    count = 2 * len(chunks)
    pieces, (win_a, win_b, wout_a, wout_b) = refs[:count], refs[count : count + 4]
    held, refs = refs[count + 4 : count + 4 + 2 * len(ahead)], refs[count + 4 + 2 * len(ahead) :]
    outs, hids = refs[: 2 * len(backs)], refs[2 * len(backs) : -2]
    rows_ref, hidden_ref = refs[-2:]
    units, width = wout_a.shape
    capacity = hids[0].shape[1]
    tile = column_tile(width)
    at = 0
    for piece in pieces:
        rows_ref[at : at + piece.shape[0]] = piece[...]
        at += piece.shape[0]
    me = me_ref[0]
    layer, chip, core = me // SLICES, (me % SLICES) // 2, me % 2
    lane_mask = (FIRST + core * (SECOND - FIRST)) // 2
    cross_mask = (SECOND - core * (SECOND - FIRST)) // 2
    masks = (0, lane_mask, cross_mask, lane_mask ^ cross_mask)
    blocks = [(s, k) for chunk in chunks for k in range(4) for s in chunk]

    def spot(s, k):
        return (layer ^ s) * CHIPS + (chip ^ masks[k])

    for e, earlier in enumerate(ahead):
        for half in (0, 1):
            for i, (s, k) in enumerate(earlier):
                hids[half][spot(s, k)] = held[2 * e + half][i]
    for half, (win, hid) in enumerate(zip((win_a, win_b), hids)):
        total = jnp.dot(rows_ref[...], win[...], preferred_element_type=jnp.float32)
        gate, up = total[:, :units], total[:, units:]
        value = (gate / (1.0 + jnp.exp(-gate)) * up).astype(jnp.bfloat16)
        hidden_ref[:, units * half : units * (half + 1)] = value
        value = value.astype(jnp.float32)
        for i, (s, k) in enumerate(blocks):
            hid[spot(s, k) if final else i] = value[
                i * capacity : (i + 1) * capacity
            ].astype(jnp.bfloat16)
    for at in range(0, width, tile):
        cols = slice(at, at + tile)
        out = jnp.dot(hidden_ref[:, :units], wout_a[:, cols], preferred_element_type=jnp.float32)
        out += jnp.dot(hidden_ref[:, units:], wout_b[:, cols], preferred_element_type=jnp.float32)
        for i, ref in enumerate(outs):
            parts = []
            for k in (0, 1) if i % 2 == 0 else (2, 3):
                for s in backs[i // 2]:
                    start = blocks.index((s, k)) * capacity
                    parts.append(out[start : start + capacity])
            ref[:, cols] = jnp.concatenate(parts, axis=0).astype(jnp.bfloat16)


def run_expert(chunks, backs, ahead, held, capacity, final, me, pieces, weights):
    width = pieces[0].shape[1]
    units = weights[2].shape[0]
    rows = sum(piece.shape[0] for piece in pieces)
    places = rows // capacity + (sum(len(earlier) for earlier in ahead) if final else 0)
    hid = jax.ShapeDtypeStruct((places, capacity, units), jnp.bfloat16)
    outs = [
        jax.ShapeDtypeStruct((2 * len(back) * capacity, width), jnp.bfloat16)
        for back in backs
        for _ in (0, 1)
    ]
    return pl.pallas_call(
        functools.partial(expert_kernel, chunks, backs, ahead, final),
        out_shape=outs + [hid] * 2,
        in_specs=[SMEM] + [VMEM] * (len(pieces) + 4 + len(held)),
        out_specs=[VMEM] * (len(outs) + 2),
        scratch_shapes=[
            pltpu.VMEM((rows, width), jnp.bfloat16),
            pltpu.VMEM((rows, 2 * units), jnp.bfloat16),
        ],
        compiler_params=pltpu.CompilerParams(vmem_limit_bytes=16 * MIB),
        cost_estimate=pl.CostEstimate(flops=1, bytes_accessed=1, transcendentals=0),
    )(me, *pieces, *weights, *held)


def weave_kernel(me_ref, mine_ref, other_ref, out_ref):
    core = me_ref[0] % 2
    out_ref[:, pl.ds(core, 1)] = mine_ref[...][:, None]
    out_ref[:, pl.ds(1 - core, 1)] = other_ref[...][:, None]


def keep_kernel(me_ref, swap_ref, mine_ref, far_ref, out_ref):
    flag = swap_ref[me_ref[0] % swap_ref.shape[0]]
    out_ref[...] = jnp.where(flag == 1, far_ref[...], mine_ref[...])


def mix_kernel(hi_ref, lo_ref, *refs):
    values, out, (stage_ref, sems) = refs[:-3], refs[-3], refs[-2:]
    width = stage_ref.shape[1]
    tile = column_tile(width)
    copies = []
    for k in range(width // tile):
        cols = pl.ds(k * tile, tile)
        rows = jnp.concatenate([r[:, cols].astype(jnp.float32) for r in values], axis=0)
        rows = rows.astype(jnp.bfloat16)
        total = jnp.dot(hi_ref[...], rows, preferred_element_type=jnp.float32)
        total += jnp.dot(lo_ref[...], rows, preferred_element_type=jnp.float32)
        stage_ref[:, cols] = total.astype(jnp.bfloat16)
        copy = pltpu.make_async_copy(stage_ref.at[:, cols], out.at[:, cols], sems.at[k])
        copy.start()
        copies.append(copy)
    for copy in copies:
        copy.wait()


GATHER = [[0], [1, 3], [2]]
BACKS = [[3], [2], [1], [0]]
GROUPS = [[0, 1], [2]]
PLAN = (
    ("Z", 3, 3), ("L", 0, 0), ("Z", 1, 0), ("W", 1, 1), ("l", 0, 0), ("X", 0, 0), ("z", 3, 3),
    ("Z", 2, 3), ("z", 1, 1), ("W", 0, 2), ("L", 1, 3), ("l", 1, 2), ("X", 1, 2), ("w", 0, 1),
    ("z", 2, 3), ("L", 2, 0), ("w", 1, 0), ("x", 0, 1), ("l", 2, 3), ("X", 2, 1), ("x", 1, 0),
    ("K", 0, 0), ("x", 2, 0), ("K", 1, 0), ("C", 2, 0), ("C", 0, 0), ("C", 1, 0), ("H", 0, 1),
    ("h", 0, 0), ("F", 0, 1), ("c", 0, 2), ("A", 0, 2), ("c", 1, 1), ("A", 1, 2), ("a", 0, 1),
    ("B", 3, 2), ("C", 3, 1), ("c", 2, 1), ("A", 2, 0), ("a", 1, 0), ("B", 2, 0), ("f", 0, 1),
    ("a", 2, 0), ("B", 1, 0), ("c", 3, 0), ("A", 3, 0), ("b", 3, 3), ("b", 2, 3), ("b", 1, 3),
    ("a", 3, 1),
)


def plain_plan(experts):
    steps = [("W", 0), ("W", 1)] + [("Z", s) for s in range(1, experts)] + [("w", 0), ("w", 1)]
    steps += [("z", s) for s in range(1, experts)]
    for s in range(experts):
        steps += [("L", s), ("l", s), ("X", s), ("x", s)]
    steps += [("K", 0), ("H", 0), ("h", 0), ("F", 0), ("f", 0)]
    for s in range(experts):
        steps += [("C", s), ("c", s), ("A", s), ("a", s)]
    steps += [("B", s) for s in range(1, experts)] + [("b", s) for s in range(1, experts)]
    return [(kind, at, 0) for kind, at in steps]


def shards(tokens, route_token, route_expert, route_gate, w_in, w_out, swap_pairs):
    devices = lax.axis_size("ep")
    half_axis = devices // 2
    tok_count, width = tokens.shape
    units = w_out.shape[1]
    rows_dev = route_token.shape[0]
    experts = devices // SLICES
    capacity = min(rows_dev, 3 * rows_dev // (2 * experts))
    places = experts * capacity
    me = lax.axis_index("ep").astype(jnp.int32).reshape(1)
    small = pltpu.CompilerParams(vmem_limit_bytes=16 * MIB)
    tuned = experts == 1 + max(max(chunk) for chunk in GATHER)
    singles = [[s] for s in range(experts)]
    chunks, backs, groups = (GATHER, BACKS, GROUPS) if tuned else (singles, singles, [list(range(experts))])
    plan = PLAN if tuned else plain_plan(experts)

    *bufs, gate_hi, gate_lo = run_route(
        experts, capacity, me, route_expert, route_token, route_gate, tokens
    )
    both_weights = [w_in[0], w_out[0]]
    flying, came, both = {}, {("z", 0): bufs[0]}, {}
    near, away, sums, held, ahead = {}, {}, {}, [], []
    token = me

    def send(key, value, mask_of, mark):
        nonlocal token
        if mark == 3:
            token, value = lax.optimization_barrier((token, value))
        elif mark == 2:
            token = after(token, value)
        elif mark == 1:
            value = after(value, token)
        flying[key] = swap(value, mask_of)

    for kind, s, mark in plan:
        if kind == "W":
            send(("w", s), both_weights[s], lambda i: CORE, mark)
        elif kind == "Z":
            send(("z", s), bufs[s], lambda i: SLICES * s, mark)
        elif kind == "L":
            both[s] = [came["z", e] for e in chunks[s]]
            mine = jnp.concatenate(both[s], axis=0) if len(both[s]) > 1 else both[s][0]
            send(("l", s), mine, lane, mark)
        elif kind == "X":
            both[s] = jnp.concatenate(both[s] + [came["l", s]], axis=0)
            send(("x", s), both[s], cross, mark)
        elif kind == "K":
            group = groups[s]
            pieces = sum([[both[c], came["x", c]] for c in group], [])
            weights = [w_in[0], came["w", 0], w_out[0], came["w", 1]]
            inside = [e for c in group for e in chunks[c]]
            mine = [i for i, back in enumerate(backs) if back[0] in inside]
            final = s == len(groups) - 1
            *outs, hid_a, hid_b = run_expert(
                [chunks[c] for c in group],
                [backs[i] for i in mine],
                ahead if final else [],
                held if final else [],
                capacity,
                final,
                me,
                pieces,
                weights,
            )
            held = held + [hid_a, hid_b]
            ahead = ahead + [[(e, k) for c in group for k in range(4) for e in chunks[c]]]
            for i, index in enumerate(mine):
                near[index], away[index] = outs[2 * i : 2 * i + 2]
        elif kind == "C":
            send(("c", s), away[s], cross, mark)
        elif kind == "A":
            half = near[s].shape[0] // 2
            relay = near[s][half:].astype(jnp.float32) + came["c", s][half:].astype(jnp.float32)
            send(("a", s), relay.astype(jnp.bfloat16), lane, mark)
        elif kind == "B":
            send(("b", s), sums[s], lambda i: SLICES * s, mark)
        elif kind == "H":
            send(("h", 0), hid_b, lambda i: CORE, mark)
        elif kind == "F":
            full = pl.pallas_call(
                weave_kernel,
                out_shape=jax.ShapeDtypeStruct((devices // 2, 2, capacity, units), jnp.bfloat16),
                in_specs=[SMEM, VMEM, VMEM],
                out_specs=VMEM,
                compiler_params=small,
            )(me, hid_a, came["h", 0])
            send(("f", 0), full, lambda i: half_axis, mark)
        else:
            value = flying[kind, s]
            if mark == 3:
                token, value = lax.optimization_barrier((token, value))
            elif mark == 2:
                token = after(token, value)
            elif mark == 1:
                value = after(value, token)
            came[kind, s] = value
            if kind == "a":
                parts = (near[s], came["c", s], came["a", s])
                for i, e in enumerate(backs[s]):
                    rows = slice(i * capacity, (i + 1) * capacity)
                    total = sum(part[rows].astype(jnp.float32) for part in parts)
                    sums[e] = total.astype(jnp.bfloat16)

    saved = pl.pallas_call(
        keep_kernel,
        out_shape=jax.ShapeDtypeStruct(full.shape, full.dtype),
        in_specs=[SMEM, SMEM, VMEM, VMEM],
        out_specs=pl.BlockSpec(),
        compiler_params=small,
    )(me, swap_pairs, full, came["f", 0])
    finals = after([sums[0]] + [came["b", s] for s in range(1, experts)], token)
    mixed = pl.pallas_call(
        mix_kernel,
        out_shape=jax.ShapeDtypeStruct((tok_count, width), jnp.bfloat16),
        in_specs=[VMEM] * (2 + experts),
        out_specs=ANY,
        scratch_shapes=[
            pltpu.VMEM((tok_count, width), jnp.bfloat16),
            pltpu.SemaphoreType.DMA((width // column_tile(width),)),
        ],
        compiler_params=small,
    )(gate_hi, gate_lo, *finals)
    return (mixed, saved.reshape(1, devices * capacity, units))


def solution(mesh):
    return jax.shard_map(
        shards,
        mesh=mesh,
        in_specs=(
            P(("rep", "ep"), None),
            P(("rep", "ep")),
            P(("rep", "ep"), None),
            P(("rep", "ep")),
            P("ep", None, None),
            P("ep", None, None),
            P(),
        ),
        out_specs=(P(("rep", "ep"), None), P(("rep", "ep"), None, None)),
        check_vma=False,
    )
```

```python
import functools

import jax
import jax.numpy as jnp
from jax import lax
from jax.experimental import pallas as pl
from jax.experimental.pallas import tpu as pltpu
from jax.sharding import PartitionSpec as P

SLICES = 8
CORE, FIRST, SECOND = 1, 2, 4
CHIPS = SLICES // 2
VMEM = pl.BlockSpec(memory_space=pltpu.VMEM)
SMEM = pl.BlockSpec(memory_space=pltpu.SMEM)
ANY = pl.BlockSpec(memory_space=pl.ANY)
MIB = 1024 * 1024


def swap(value, mask_of):
    count = lax.axis_size("ep")
    return lax.ppermute(value, "ep", [(i, i ^ mask_of(i)) for i in range(count)])


def after(value, others):
    return lax.optimization_barrier((value, others))[0]


def lane(i):
    return FIRST if i & CORE == 0 else SECOND


def cross(i):
    return SECOND if i & CORE == 0 else FIRST


def column_tile(width):
    return next(t for t in (1792, 512, 256, 128, width) if width % t == 0)


def route_kernel(experts, capacity, me_ref, expert_hbm, token_hbm, gate_hbm, tok_hbm, *refs):
    bufs, (hi_ref, lo_ref) = refs[:experts], refs[experts : experts + 2]
    expert_ref, token_ref, gate_ref, tok_ref, sems = refs[experts + 2 :]
    rows = expert_ref.shape[1]
    tok_count, width = tok_ref.shape
    places = experts * capacity
    tile = column_tile(width)
    tiles = width // tile
    small = [
        pltpu.make_async_copy(source, target, sems.at[i])
        for i, (source, target) in enumerate(
            ((expert_hbm, expert_ref), (token_hbm, token_ref), (gate_hbm, gate_ref))
        )
    ]
    large = [
        pltpu.make_async_copy(
            tok_hbm.at[:, pl.ds(k * tile, tile)], tok_ref.at[:, pl.ds(k * tile, tile)], sems.at[3 + k]
        )
        for k in range(tiles)
    ]
    for copy in small + large:
        copy.start()
    for copy in small:
        copy.wait()
    relative = expert_ref[...] ^ (me_ref[0] // SLICES)
    ranks = -(-experts // 8) * 8
    hits = (lax.broadcasted_iota(jnp.int32, (ranks, rows), 0) == relative).astype(jnp.float32)
    earlier = lax.broadcasted_iota(jnp.int32, (rows, rows), 0) < lax.broadcasted_iota(
        jnp.int32, (rows, rows), 1
    )
    before = jnp.dot(
        hits.astype(jnp.bfloat16),
        earlier.astype(jnp.float32).astype(jnp.bfloat16),
        preferred_element_type=jnp.float32,
    )
    slot = jnp.sum(hits * before, axis=0, keepdims=True).astype(jnp.int32)
    target = relative * capacity + slot
    place_hot = lax.broadcasted_iota(jnp.int32, (places, rows), 0) == target
    place_hot = place_hot.astype(jnp.float32).astype(jnp.bfloat16)
    token_hot = lax.broadcasted_iota(jnp.int32, (tok_count, rows), 0) == token_ref[...]
    token_hot = token_hot.astype(jnp.float32)
    contract = (((1,), (1,)), ((), ()))
    pick = lax.dot_general(
        place_hot, token_hot.astype(jnp.bfloat16), contract, preferred_element_type=jnp.float32
    ).astype(jnp.bfloat16)
    gate = gate_ref[...]
    gate_hi = gate.astype(jnp.bfloat16).astype(jnp.float32)
    for part, ref in ((gate_hi, hi_ref), (gate - gate_hi, lo_ref)):
        ref[...] = lax.dot_general(
            (token_hot * part).astype(jnp.bfloat16),
            place_hot,
            contract,
            preferred_element_type=jnp.float32,
        ).astype(jnp.bfloat16)
    for k in range(tiles):
        cols = pl.ds(k * tile, tile)
        large[k].wait()
        picked = jnp.dot(pick, tok_ref[:, cols], preferred_element_type=jnp.float32)
        for s in range(experts):
            bufs[s][:, cols] = picked[s * capacity : (s + 1) * capacity].astype(jnp.bfloat16)


def run_route(experts, capacity, me, route_expert, route_token, route_gate, tokens):
    tok_count, width = tokens.shape
    rows = route_token.shape[0]
    block = jax.ShapeDtypeStruct((capacity, width), jnp.bfloat16)
    mix = jax.ShapeDtypeStruct((tok_count, experts * capacity), jnp.bfloat16)
    return pl.pallas_call(
        functools.partial(route_kernel, experts, capacity),
        out_shape=[block] * experts + [mix] * 2,
        in_specs=[SMEM] + [ANY] * 4,
        out_specs=[VMEM] * (experts + 2),
        scratch_shapes=[
            pltpu.VMEM((1, rows), jnp.int32),
            pltpu.VMEM((1, rows), jnp.int32),
            pltpu.VMEM((1, rows), jnp.float32),
            pltpu.VMEM((tok_count, width), jnp.bfloat16),
            pltpu.SemaphoreType.DMA((3 + width // column_tile(width),)),
        ],
        compiler_params=pltpu.CompilerParams(vmem_limit_bytes=60 * MIB),
    )(
        me,
        route_expert.reshape(1, rows),
        route_token.reshape(1, rows),
        route_gate.reshape(1, rows),
        tokens,
    )


def expert_kernel(chunks, backs, ahead, final, me_ref, *refs):
    count = 2 * len(chunks)
    pieces, (win_a, win_b, wout_a, wout_b) = refs[:count], refs[count : count + 4]
    held, refs = refs[count + 4 : count + 4 + 2 * len(ahead)], refs[count + 4 + 2 * len(ahead) :]
    outs, hids = refs[: 2 * len(backs)], refs[2 * len(backs) : -2]
    rows_ref, hidden_ref = refs[-2:]
    units, width = wout_a.shape
    capacity = hids[0].shape[1]
    tile = column_tile(width)
    at = 0
    for piece in pieces:
        rows_ref[at : at + piece.shape[0]] = piece[...]
        at += piece.shape[0]
    me = me_ref[0]
    layer, chip, core = me // SLICES, (me % SLICES) // 2, me % 2
    lane_mask = (FIRST + core * (SECOND - FIRST)) // 2
    cross_mask = (SECOND - core * (SECOND - FIRST)) // 2
    masks = (0, lane_mask, cross_mask, lane_mask ^ cross_mask)
    blocks = [(s, k) for chunk in chunks for k in range(4) for s in chunk]

    def spot(s, k):
        return (layer ^ s) * CHIPS + (chip ^ masks[k])

    for e, earlier in enumerate(ahead):
        for half in (0, 1):
            for i, (s, k) in enumerate(earlier):
                hids[half][spot(s, k)] = held[2 * e + half][i]
    for half, (win, hid) in enumerate(zip((win_a, win_b), hids)):
        total = jnp.dot(rows_ref[...], win[...], preferred_element_type=jnp.float32)
        gate, up = total[:, :units], total[:, units:]
        value = (gate / (1.0 + jnp.exp(-gate)) * up).astype(jnp.bfloat16)
        hidden_ref[:, units * half : units * (half + 1)] = value
        value = value.astype(jnp.float32)
        for i, (s, k) in enumerate(blocks):
            hid[spot(s, k) if final else i] = value[
                i * capacity : (i + 1) * capacity
            ].astype(jnp.bfloat16)
    for at in range(0, width, tile):
        cols = slice(at, at + tile)
        out = jnp.dot(hidden_ref[:, :units], wout_a[:, cols], preferred_element_type=jnp.float32)
        out += jnp.dot(hidden_ref[:, units:], wout_b[:, cols], preferred_element_type=jnp.float32)
        for i, ref in enumerate(outs):
            parts = []
            for k in (0, 1) if i % 2 == 0 else (2, 3):
                for s in backs[i // 2]:
                    start = blocks.index((s, k)) * capacity
                    parts.append(out[start : start + capacity])
            ref[:, cols] = jnp.concatenate(parts, axis=0).astype(jnp.bfloat16)


def run_expert(chunks, backs, ahead, held, capacity, final, me, pieces, weights):
    width = pieces[0].shape[1]
    units = weights[2].shape[0]
    rows = sum(piece.shape[0] for piece in pieces)
    places = rows // capacity + (sum(len(earlier) for earlier in ahead) if final else 0)
    hid = jax.ShapeDtypeStruct((places, capacity, units), jnp.bfloat16)
    outs = [
        jax.ShapeDtypeStruct((2 * len(back) * capacity, width), jnp.bfloat16)
        for back in backs
        for _ in (0, 1)
    ]
    return pl.pallas_call(
        functools.partial(expert_kernel, chunks, backs, ahead, final),
        out_shape=outs + [hid] * 2,
        in_specs=[SMEM] + [VMEM] * (len(pieces) + 4 + len(held)),
        out_specs=[VMEM] * (len(outs) + 2),
        scratch_shapes=[
            pltpu.VMEM((rows, width), jnp.bfloat16),
            pltpu.VMEM((rows, 2 * units), jnp.bfloat16),
        ],
        compiler_params=pltpu.CompilerParams(vmem_limit_bytes=16 * MIB),
        cost_estimate=pl.CostEstimate(flops=1, bytes_accessed=1, transcendentals=0),
    )(me, *pieces, *weights, *held)


def weave_kernel(me_ref, mine_ref, other_ref, out_ref):
    core = me_ref[0] % 2
    out_ref[:, pl.ds(core, 1)] = mine_ref[...][:, None]
    out_ref[:, pl.ds(1 - core, 1)] = other_ref[...][:, None]


def keep_kernel(me_ref, swap_ref, mine_ref, far_ref, out_ref):
    flag = swap_ref[me_ref[0] % swap_ref.shape[0]]
    out_ref[...] = jnp.where(flag == 1, far_ref[...], mine_ref[...])


def mix_kernel(hi_ref, lo_ref, *refs):
    values, out, (stage_ref, sems) = refs[:-3], refs[-3], refs[-2:]
    width = stage_ref.shape[1]
    tile = width // sems.shape[0]
    copies = []
    for k in range(width // tile):
        cols = pl.ds(k * tile, tile)
        rows = jnp.concatenate([r[:, cols].astype(jnp.float32) for r in values], axis=0)
        rows = rows.astype(jnp.bfloat16)
        total = jnp.dot(hi_ref[...], rows, preferred_element_type=jnp.float32)
        total += jnp.dot(lo_ref[...], rows, preferred_element_type=jnp.float32)
        stage_ref[:, cols] = total.astype(jnp.bfloat16)
        copy = pltpu.make_async_copy(stage_ref.at[:, cols], out.at[:, cols], sems.at[k])
        copy.start()
        copies.append(copy)
    for copy in copies:
        copy.wait()


GATHER = [[0], [1, 3], [2]]
BACKS = [[3], [2], [1], [0]]
GROUPS = [[0, 1], [2]]
PLAN = (
    ("Z", 3, 3), ("L", 0, 0), ("Z", 1, 0), ("W", 1, 1), ("l", 0, 0), ("X", 0, 0), ("z", 3, 3),
    ("Z", 2, 3), ("z", 1, 1), ("W", 0, 2), ("L", 1, 3), ("l", 1, 2), ("X", 1, 2), ("w", 0, 1),
    ("z", 2, 3), ("L", 2, 0), ("w", 1, 0), ("x", 0, 1), ("l", 2, 3), ("X", 2, 1), ("x", 1, 0),
    ("K", 0, 0), ("x", 2, 0), ("K", 1, 0), ("C", 2, 0), ("C", 0, 0), ("C", 1, 0), ("H", 0, 1),
    ("h", 0, 0), ("F", 0, 1), ("c", 0, 2), ("A", 0, 2), ("c", 1, 1), ("A", 1, 2), ("a", 0, 1),
    ("B", 3, 2), ("C", 3, 1), ("c", 2, 1), ("A", 2, 0), ("a", 1, 0), ("B", 2, 0), ("f", 0, 1),
    ("a", 2, 0), ("B", 1, 0), ("c", 3, 0), ("A", 3, 0), ("b", 3, 3), ("b", 2, 3), ("b", 1, 3),
    ("a", 3, 1),
)


def plain_plan(experts):
    steps = [("W", 0), ("W", 1)] + [("Z", s) for s in range(1, experts)] + [("w", 0), ("w", 1)]
    steps += [("z", s) for s in range(1, experts)]
    for s in range(experts):
        steps += [("L", s), ("l", s), ("X", s), ("x", s)]
    steps += [("K", 0), ("H", 0), ("h", 0), ("F", 0), ("f", 0)]
    for s in range(experts):
        steps += [("C", s), ("c", s), ("A", s), ("a", s)]
    steps += [("B", s) for s in range(1, experts)] + [("b", s) for s in range(1, experts)]
    return [(kind, at, 0) for kind, at in steps]


def shards(tokens, route_token, route_expert, route_gate, w_in, w_out, swap_pairs):
    devices = lax.axis_size("ep")
    half_axis = devices // 2
    tok_count, width = tokens.shape
    units = w_out.shape[1]
    rows_dev = route_token.shape[0]
    experts = devices // SLICES
    capacity = min(rows_dev, 3 * rows_dev // (2 * experts))
    places = experts * capacity
    me = lax.axis_index("ep").astype(jnp.int32).reshape(1)
    small = pltpu.CompilerParams(vmem_limit_bytes=16 * MIB)
    tuned = experts == 1 + max(max(chunk) for chunk in GATHER)
    singles = [[s] for s in range(experts)]
    chunks, backs, groups = (GATHER, BACKS, GROUPS) if tuned else (singles, singles, [list(range(experts))])
    plan = PLAN if tuned else plain_plan(experts)

    *bufs, gate_hi, gate_lo = run_route(
        experts, capacity, me, route_expert, route_token, route_gate, tokens
    )
    both_weights = [w_in[0], w_out[0]]
    flying, came, both = {}, {("z", 0): bufs[0]}, {}
    near, away, sums, held, ahead = {}, {}, {}, [], []
    token = me

    def send(key, value, mask_of, mark):
        nonlocal token
        if mark == 3:
            token, value = lax.optimization_barrier((token, value))
        elif mark == 2:
            token = after(token, value)
        elif mark == 1:
            value = after(value, token)
        flying[key] = swap(value, mask_of)

    for kind, s, mark in plan:
        if kind == "W":
            send(("w", s), both_weights[s], lambda i: CORE, mark)
        elif kind == "Z":
            send(("z", s), bufs[s], lambda i: SLICES * s, mark)
        elif kind == "L":
            both[s] = [came["z", e] for e in chunks[s]]
            mine = jnp.concatenate(both[s], axis=0) if len(both[s]) > 1 else both[s][0]
            send(("l", s), mine, lane, mark)
        elif kind == "X":
            both[s] = jnp.concatenate(both[s] + [came["l", s]], axis=0)
            send(("x", s), both[s], cross, mark)
        elif kind == "K":
            group = groups[s]
            pieces = sum([[both[c], came["x", c]] for c in group], [])
            weights = [w_in[0], came["w", 0], w_out[0], came["w", 1]]
            inside = [e for c in group for e in chunks[c]]
            mine = [i for i, back in enumerate(backs) if back[0] in inside]
            final = s == len(groups) - 1
            *outs, hid_a, hid_b = run_expert(
                [chunks[c] for c in group],
                [backs[i] for i in mine],
                ahead if final else [],
                held if final else [],
                capacity,
                final,
                me,
                pieces,
                weights,
            )
            held = held + [hid_a, hid_b]
            ahead = ahead + [[(e, k) for c in group for k in range(4) for e in chunks[c]]]
            for i, index in enumerate(mine):
                near[index], away[index] = outs[2 * i : 2 * i + 2]
        elif kind == "C":
            send(("c", s), away[s], cross, mark)
        elif kind == "A":
            half = near[s].shape[0] // 2
            relay = near[s][half:].astype(jnp.float32) + came["c", s][half:].astype(jnp.float32)
            send(("a", s), relay.astype(jnp.bfloat16), lane, mark)
        elif kind == "B":
            send(("b", s), sums[s], lambda i: SLICES * s, mark)
        elif kind == "H":
            send(("h", 0), hid_b, lambda i: CORE, mark)
        elif kind == "F":
            full = pl.pallas_call(
                weave_kernel,
                out_shape=jax.ShapeDtypeStruct((devices // 2, 2, capacity, units), jnp.bfloat16),
                in_specs=[SMEM, VMEM, VMEM],
                out_specs=VMEM,
                compiler_params=small,
            )(me, hid_a, came["h", 0])
            send(("f", 0), full, lambda i: half_axis, mark)
        else:
            value = flying[kind, s]
            if mark == 3:
                token, value = lax.optimization_barrier((token, value))
            elif mark == 2:
                token = after(token, value)
            elif mark == 1:
                value = after(value, token)
            came[kind, s] = value
            if kind == "a":
                parts = (near[s], came["c", s], came["a", s])
                for i, e in enumerate(backs[s]):
                    rows = slice(i * capacity, (i + 1) * capacity)
                    total = sum(part[rows].astype(jnp.float32) for part in parts)
                    sums[e] = total.astype(jnp.bfloat16)

    saved = pl.pallas_call(
        keep_kernel,
        out_shape=jax.ShapeDtypeStruct(full.shape, full.dtype),
        in_specs=[SMEM, SMEM, VMEM, VMEM],
        out_specs=pl.BlockSpec(),
        compiler_params=small,
    )(me, swap_pairs, full, came["f", 0])
    finals = after([sums[0]] + [came["b", s] for s in range(1, experts)], token)
    mixed = pl.pallas_call(
        mix_kernel,
        out_shape=jax.ShapeDtypeStruct((tok_count, width), jnp.bfloat16),
        in_specs=[VMEM] * (2 + experts),
        out_specs=ANY,
        scratch_shapes=[
            pltpu.VMEM((tok_count, width), jnp.bfloat16),
            pltpu.SemaphoreType.DMA((max(1, width // 896),)),
        ],
        compiler_params=small,
    )(gate_hi, gate_lo, *finals)
    return (mixed, saved.reshape(1, devices * capacity, units))


def solution(mesh):
    return jax.shard_map(
        shards,
        mesh=mesh,
        in_specs=(
            P(("rep", "ep"), None),
            P(("rep", "ep")),
            P(("rep", "ep"), None),
            P(("rep", "ep")),
            P("ep", None, None),
            P("ep", None, None),
            P(),
        ),
        out_specs=(P(("rep", "ep"), None), P(("rep", "ep"), None, None)),
        check_vma=False,
    )
```
